32 devices in a mesh: bpar: 2 (over y), tgt: 4 (over z), prj: 2 (over x), rep: 2 (over core).
Axes of the slice: x: 2, y: 2, z: 4, core: 2. Of those that a mesh axis runs over, the one named last changes fastest.
Arguments:
- tgt_basis: bfloat16 [2, 4096, 512], P(None, 'tgt', 'rep'), may hold values from -6 to 6
- proj_basis: bfloat16 [2, 8, 512, 512], P(None, None, 'prj', 'rep'), may hold values from -0.00390625 to 0.00390625
- quad_weight: float32 [1024], P(('bpar', 'rep')), parts along dimension 0, may hold values from 0.3 to 3
- tgt_energy: float32 [4096], P(('tgt', 'prj', 'rep')), may hold values from -1 to 1
- proj_energy: float32 [8, 512], P(('tgt', 'rep'), 'prj'), may hold values from -1 to 1
- pair_flags: int32 [8, 2], P('bpar'), parts along dimension 0, may hold values 0 or 1
- tile_counts: int32 [8, 2], P('bpar'), parts along dimension 0, may hold values from 1 to 4
- tgt_amp: float32 [8192, 128], P(('bpar', 'tgt', 'prj', 'rep')), parts along dimension 0, may hold values from -6 to 6
- proj_amp: float32 [16, 512, 128], P(('bpar', 'tgt', 'rep'), 'prj'), parts along dimension 0, may hold values from -6 to 6
Outputs:
- new_tgt_amp: float32 [8192, 128], P(('bpar', 'tgt', 'prj', 'rep')), parts along dimension 0
- new_proj_amp: float32 [16, 512, 128], P(('bpar', 'tgt', 'rep'), 'prj'), parts along dimension 0
The draws below stay inside these ranges and needn't reach their ends.
There are 2 independent parts, one for each index of `bpar`. The reference program is written for one: setup_inputs(seed, part) draws one part's arguments, and reference() takes and returns one part's arrays. A program takes and returns all parts, laid end to end along the dimension named above; an argument that names none is the same for every part. Nothing has to cross between parts.
All inputs are finite; a program needn't handle non-finite values.
Results may differ from the reference program's by a relative error of at most 0.02.
Values may be sent and summed in bfloat16 or wider, within the bound.
A program may use at most 64 MiB of HBM per device.

```python
import math
import jax
import jax.numpy as jnp
from jax import lax

TSD = 1024
PSD = 2048
QUAD = 512
COLS = 64
QTILE = 128
TS = 4096
SUBS = 8
PROWS = 256
N_TGT = 4
N_PRJ = 2


def plant(values, rng, smallest, high):
    dims = values.shape
    spot = [jax.random.randint(jax.random.fold_in(rng, axis), (), 0, dims[axis]) for axis in range(len(dims))]
    values = values.at[tuple(spot)].set(smallest)
    longest = dims.index(max(dims))
    spot[longest] = (spot[longest] + 1) % dims[longest]
    return values.at[tuple(spot)].set(high)


def steps_of(rng, dims, pieces, smallest, largest):
    gain = 1.0
    for dim, shards_of in pieces:
        heights = jax.random.uniform(jax.random.fold_in(jax.random.fold_in(rng, 6), dim), (shards_of,), jnp.float32, smallest / len(pieces), largest / len(pieces))
        gain = gain * jnp.repeat(jnp.exp(heights), dims[dim] // shards_of).reshape((-1,) + (1,) * (len(dims) - 1 - dim))
    return gain


def gaussian(key, dims, spread, limit, split=(), held_as=jnp.bfloat16):
    loudness = steps_of(key, dims, split, -0.22, 0.18) if split else 1.0
    entries = jax.random.normal(key, dims, jnp.float32) * spread * loudness
    return jnp.minimum(jnp.maximum(entries, -limit), limit).astype(held_as)


def setup_inputs(seed: int = 0, part: int = 0) -> dict:
    keys = jax.random.split(jax.random.key(seed), 10)
    part_keys = jax.random.split(jax.random.fold_in(keys[9], part), 10)
    tgt_basis = gaussian(keys[0], (2, TS, QUAD), 1.0, 6.0, ((1, 4), (2, 2)))
    proj_basis = gaussian(keys[1], (2, SUBS, PROWS * N_PRJ, QUAD), (QUAD * PSD * N_PRJ) ** -0.5, 0.00390625, ((2, 2), (3, 2)))
    quad_weight = jnp.clip(jnp.exp(math.log(3.0) - 2.3025851 * jax.random.uniform(part_keys[2], (QUAD,), jnp.float32) ** steps_of(part_keys[2], (QUAD,), ((0, 2),), -0.2, 0.2)), 0.3, 3.0)
    tgt_energy = jnp.clip(jax.random.uniform(keys[3], (TS,), jnp.float32, -1.0, 1.0) * steps_of(keys[3], (TS,), ((0, 16),), -0.4, 0.0), -1.0, 1.0)
    proj_energy = jnp.clip(jax.random.uniform(keys[4], (SUBS, PROWS * N_PRJ), jnp.float32, -1.0, 1.0) * steps_of(keys[4], (SUBS, PROWS * N_PRJ), ((0, 8), (1, 2)), -0.4, 0.0), -1.0, 1.0)
    pair_flags = plant((jax.random.randint(part_keys[5], (N_TGT, N_PRJ), 0, 3) < 2).astype(jnp.int32), jax.random.fold_in(part_keys[5], 1), 0, 1)
    tile_counts = plant(jax.random.randint(part_keys[6], (N_TGT, N_PRJ), 1, 5), jax.random.fold_in(part_keys[6], 1), 1, 4).astype(jnp.int32)
    tgt_amp = gaussian(part_keys[7], (TS, 2 * COLS), 1.0, 6.0, ((0, 16),), jnp.float32)
    proj_amp = gaussian(part_keys[8], (SUBS, PROWS * N_PRJ, 2 * COLS), 1.0, 6.0, ((0, 8), (1, 2)), jnp.float32)
    return dict(tgt_basis=tgt_basis, proj_basis=proj_basis, quad_weight=quad_weight, tgt_energy=tgt_energy, proj_energy=proj_energy, pair_flags=pair_flags, tile_counts=tile_counts, tgt_amp=tgt_amp, proj_amp=proj_amp)


time_step = 0.4


def rotate(energy, state_now, coupled):
    half_cols = state_now.shape[-1] // 2
    summed = energy[..., None] * state_now + coupled
    return jnp.concatenate([summed[..., half_cols:], -summed[..., :half_cols]], axis=-1)


def round_trip(values):
    return lax.optimization_barrier(values.astype(jnp.bfloat16)).astype(jnp.float32)


def pairwise_product(form, left_side, right_side):
    return jnp.einsum(form, left_side, right_side, precision=lax.Precision.HIGHEST)


def coupled_rates(tgt_state, proj_state, tgt_energy, proj_energy, target_real, target_imag, projectile_part_real, projectile_part_imag, weights, live_state_mask):
    tgt_send = round_trip(tgt_state).reshape(N_TGT, TSD, 2 * COLS)
    proj_send = round_trip(proj_state).reshape(SUBS, N_PRJ, PROWS, 2 * COLS)
    amp_real = tgt_send[..., :COLS]
    amp_imag = tgt_send[..., COLS:]
    coef_real = pairwise_product('aiq,aik->aqk', target_real, amp_real) + pairwise_product('aiq,aik->aqk', target_imag, amp_imag)
    coef_imag = pairwise_product('aiq,aik->aqk', target_real, amp_imag) - pairwise_product('aiq,aik->aqk', target_imag, amp_real)
    target_coefficient = round_trip(weights[None, :, None] * jnp.concatenate([coef_real, coef_imag], axis=-1))
    projectile_amplitude_real = proj_send[..., :COLS]
    projectile_amplitude_imag = proj_send[..., COLS:]
    projectile_coefficient_real = pairwise_product('xyvi,xyvt->yit', projectile_part_real, projectile_amplitude_real) + pairwise_product('xyvi,xyvt->yit', projectile_part_imag, projectile_amplitude_imag)
    projectile_coefficient_imag = pairwise_product('xyvi,xyvt->yit', projectile_part_real, projectile_amplitude_imag) - pairwise_product('xyvi,xyvt->yit', projectile_part_imag, projectile_amplitude_real)
    projectile_coefficient = round_trip(weights[None, :, None] * jnp.concatenate([projectile_coefficient_real, projectile_coefficient_imag], axis=-1))
    target_field = pairwise_product('mhg,hge->mge', live_state_mask, projectile_coefficient)
    projectile_field = pairwise_product('nod,ndm->odm', live_state_mask, target_coefficient)
    field_real = target_field[..., :COLS]
    field_imag = target_field[..., COLS:]
    yt_real = pairwise_product('aiq,aqk->aik', target_real, field_real) - pairwise_product('aiq,aqk->aik', target_imag, field_imag)
    yt_imag = pairwise_product('aiq,aqk->aik', target_real, field_imag) + pairwise_product('aiq,aqk->aik', target_imag, field_real)
    tgt_coupled = jnp.concatenate([yt_real, yt_imag], axis=-1).reshape(TS, 2 * COLS)
    projectile_field_real = projectile_field[..., :COLS]
    projectile_field_imag = projectile_field[..., COLS:]
    midpoint_projectile_real = pairwise_product('lvpf,vfw->lvpw', projectile_part_real, projectile_field_real) - pairwise_product('lvpf,vfw->lvpw', projectile_part_imag, projectile_field_imag)
    midpoint_projectile_imag = pairwise_product('lvpf,vfw->lvpw', projectile_part_real, projectile_field_imag) + pairwise_product('lvpf,vfw->lvpw', projectile_part_imag, projectile_field_real)
    proj_coupled = jnp.concatenate([midpoint_projectile_real, midpoint_projectile_imag], axis=-1).reshape(SUBS, N_PRJ * PROWS, 2 * COLS)
    return rotate(tgt_energy, tgt_state, tgt_coupled), rotate(proj_energy, proj_state, proj_coupled)


def reference(tgt_basis, proj_basis, quad_weight, tgt_energy, proj_energy, pair_flags, tile_counts, tgt_amp, proj_amp):
    target_all = tgt_basis.astype(jnp.float32).reshape(2, N_TGT, TSD, QUAD)
    projectile_all = proj_basis.astype(jnp.float32).reshape(2, SUBS, N_PRJ, PROWS, QUAD)
    tile_of = jnp.arange(QUAD, dtype=jnp.int32) // QTILE
    live_state_mask = jnp.logical_and(tile_of[None, None, :] < tile_counts[:, :, None], pair_flags[:, :, None] > 0).astype(jnp.float32)

    def rates_at(tgt_state, proj_state):
        return coupled_rates(tgt_state, proj_state, tgt_energy, proj_energy, target_all[0], target_all[1], projectile_all[0], projectile_all[1], quad_weight, live_state_mask)

    tgt_rate, proj_rate = rates_at(tgt_amp, proj_amp)
    tgt_half = tgt_amp + 0.5 * time_step * tgt_rate
    proj_half = proj_amp + 0.5 * time_step * proj_rate
    tgt_rate, proj_rate = rates_at(tgt_half, proj_half)
    return tgt_amp + time_step * tgt_rate, proj_amp + time_step * proj_rate
```

```python
import functools

import jax
import jax.numpy as jnp
from jax import lax
from jax.experimental import pallas as pl
from jax.experimental.pallas import tpu as pltpu
from jax.sharding import PartitionSpec as P

time_step = 0.4


def rotate(energy, state_now, coupled):
    half_cols = state_now.shape[-1] // 2
    summed = energy[..., None] * state_now + coupled
    return jnp.concatenate([summed[..., half_cols:], -summed[..., :half_cols]], axis=-1)


def turned(amplitude):
    half_cols = amplitude.shape[-1] // 2
    return jnp.concatenate([amplitude[..., half_cols:], -amplitude[..., :half_cols]], axis=-1)


def conj_project(basis_real, basis_imag, amplitude):
    contract = (((0,), (0,)), ((), ()))
    first_part = lax.dot_general(
        basis_real, amplitude, contract, preferred_element_type=jnp.float32
    )
    second = lax.dot_general(
        basis_imag, turned(amplitude), contract, preferred_element_type=jnp.float32
    )
    return first_part + second


def expand(basis_real, basis_imag, projected):
    first_part = jnp.dot(basis_real, projected, preferred_element_type=jnp.float32)
    second = jnp.dot(basis_imag, turned(projected), preferred_element_type=jnp.float32)
    return first_part - second


def shards(
    tgt_basis,
    proj_basis,
    quad_weight,
    tgt_energy,
    proj_energy,
    pair_flags,
    tile_counts,
    tgt_amp,
    proj_amp,
):
    rep_index = lax.axis_index("rep")
    tgt_index = lax.axis_index("tgt")
    prj_index = lax.axis_index("prj")
    pair_flag = pair_flags[tgt_index, prj_index]
    pair_tiles = tile_counts[tgt_index, prj_index]
    tile_width = quad_weight.shape[0] // 2
    lower_tiles = (
        tgt_basis[..., :tile_width],
        proj_basis[..., :tile_width],
        quad_weight[:tile_width],
    )
    upper_tiles = (
        tgt_basis[..., tile_width:],
        proj_basis[..., tile_width:],
        quad_weight[tile_width:],
    )
    first_tiles = list(lower_tiles)
    second_tiles = list(upper_tiles)
    tile_ids = (2 * rep_index, 2 * rep_index + 1)
    slot_list = []
    for tile_id, tile_set in zip(tile_ids, (first_tiles, second_tiles)):
        is_live = jnp.logical_and(pair_flag > 0, tile_id < pair_tiles)
        slot_list.append((is_live, tile_set[0], tile_set[1], tile_set[2]))

    def coupled_rates(tgt_state, proj_state):
        tgt_send = tgt_state.astype(jnp.bfloat16)
        proj_send = proj_state.astype(jnp.bfloat16)
        two_cols = tgt_state.shape[-1]
        group_rows = proj_state.shape[1]
        zero_block = jnp.zeros((tile_width, two_cols), jnp.float32)
        shard_rows = lax.all_gather(tgt_send, ("prj", "rep"), axis=0, tiled=True)
        row_count = shard_rows.shape[0]
        updated = []
        for add_slot_index in range(2):
            is_live, tgt_tile = (slot_list[add_slot_index][0], slot_list[add_slot_index][1])
            basis_real = tgt_tile[0]
            basis_imag = tgt_tile[1]
            term = lax.cond(
                is_live,
                lambda: conj_project(basis_real, basis_imag, shard_rows),
                lambda: zero_block,
            )
            updated.append(term)
        tgt_raw = (updated[0], updated[1])
        target_coefficient = [
            (slot_list[slot_index][3][:, None] * tgt_raw[slot_index]).astype(jnp.bfloat16)
            for slot_index in range(2)
        ]

        def add_projectile(shard_rows):
            row_count = shard_rows.shape[0]
            flat_rows = shard_rows.reshape(row_count * group_rows, two_cols)
            updated = []
            for slot_index in range(2):
                is_live, proj_tile = (slot_list[slot_index][0], slot_list[slot_index][2])
                basis_real = proj_tile[0].reshape(row_count * group_rows, tile_width)
                basis_imag = proj_tile[1].reshape(row_count * group_rows, tile_width)
                term = lax.cond(
                    is_live,
                    lambda: conj_project(basis_real, basis_imag, flat_rows),
                    lambda: zero_block,
                )
                updated.append(term)
            return (updated[0], updated[1])

        proj_raw = add_projectile(lax.all_gather(proj_send, ("tgt", "rep"), axis=0, tiled=True))
        projectile_coefficient = [
            (slot_list[slot_index][3][:, None] * proj_raw[slot_index]).astype(jnp.bfloat16)
            for slot_index in range(2)
        ]
        row_count = proj_state.shape[0] * lax.axis_size(("tgt", "rep"))
        zero_terms = jnp.zeros((row_count, group_rows, two_cols), jnp.float32)
        summed = zero_terms
        for slot_index in range(2):
            is_live, proj_tile = (slot_list[slot_index][0], slot_list[slot_index][2])
            projectile_basis_real = proj_tile[0].reshape(row_count * group_rows, tile_width)
            projectile_basis_imag = proj_tile[1].reshape(row_count * group_rows, tile_width)
            coef_now = target_coefficient[slot_index]
            term = lax.cond(
                is_live,
                lambda: expand(projectile_basis_real, projectile_basis_imag, coef_now).reshape(
                    row_count, group_rows, two_cols
                ),
                lambda: zero_terms,
            )
            summed = summed + term
        proj_coupled = lax.psum_scatter(
            summed.astype(jnp.bfloat16), ("tgt", "rep"), scatter_dimension=0, tiled=True
        ).astype(jnp.float32)
        target_zero_terms = jnp.zeros(
            (tgt_state.shape[0] * lax.axis_size(("prj", "rep")), two_cols), jnp.float32
        )
        summed = target_zero_terms
        for slot_index in range(2):
            is_live, tgt_tile = (slot_list[slot_index][0], slot_list[slot_index][1])
            target_basis_real = tgt_tile[0]
            target_basis_imag = tgt_tile[1]
            target_coef_now = projectile_coefficient[slot_index]
            term = lax.cond(
                is_live,
                lambda: expand(target_basis_real, target_basis_imag, target_coef_now),
                lambda: target_zero_terms,
            )
            summed = summed + term
        tgt_coupled = lax.psum_scatter(
            summed.astype(jnp.bfloat16), ("prj", "rep"), scatter_dimension=0, tiled=True
        ).astype(jnp.float32)
        return (
            rotate(tgt_energy, tgt_state, tgt_coupled),
            rotate(proj_energy, proj_state, proj_coupled),
        )

    tgt_rate, proj_rate = coupled_rates(tgt_amp, proj_amp)
    tgt_half = tgt_amp + 0.5 * time_step * tgt_rate
    proj_half = proj_amp + 0.5 * time_step * proj_rate
    tgt_rate, proj_rate = coupled_rates(tgt_half, proj_half)
    return (tgt_amp + time_step * tgt_rate, proj_amp + time_step * proj_rate)


def half_turn(values):
    half = values.shape[0] // 2
    return jnp.concatenate([values[half:], -values[:half]], axis=0)


def step_kernel(
    n_tgt,
    n_prj,
    tgt_basis,
    proj_basis,
    quad_weight,
    tgt_energy,
    proj_energy,
    flags,
    counts,
    tgt_amp,
    proj_amp,
    tgt_out,
    proj_out,
    tgt_tiles,
    proj_tiles,
    weight,
    energy,
    raw,
    state,
    masked,
    z_send,
    z_recv,
    f_send,
    f_recv,
    y_send,
    y_recv,
    load_sem,
    init_send_sem,
    init_recv_sem,
    z_send_sem,
    z_recv_sem,
    f_send_sem,
    f_recv_sem,
    y_send_sem,
    y_recv_sem,
):
    n = n_tgt * n_prj
    a, b, r = lax.axis_index("tgt"), lax.axis_index("prj"), lax.axis_index("rep")
    me = a * n_prj + b
    rows = tgt_amp.shape[0]
    points = quad_weight.shape[1]
    two_cols = tgt_amp.shape[1]
    deltas = [(da, db) for da in range(n_tgt) for db in range(n_prj)]
    core = {"rep": 1 - r}

    def chip(delta):
        return {"tgt": lax.bitwise_xor(a, delta[0]), "prj": lax.bitwise_xor(b, delta[1])}

    def chip_index(delta):
        return lax.bitwise_xor(a, delta[0]) * n_prj + lax.bitwise_xor(b, delta[1])

    loads = [
        pltpu.make_async_copy(tgt_amp, raw.at[0, 0], load_sem.at[0]),
        pltpu.make_async_copy(proj_amp.at[0], raw.at[1, 0], load_sem.at[1]),
        pltpu.make_async_copy(tgt_energy, energy.at[0, 0], load_sem.at[2]),
        pltpu.make_async_copy(proj_energy, energy.at[1, 0], load_sem.at[3]),
        pltpu.make_async_copy(quad_weight, weight, load_sem.at[4]),
    ]
    for half in range(2):
        own = r if half == 0 else 1 - r
        start = pl.multiple_of((b * 2 + own) * rows, rows)
        loads.append(
            pltpu.make_async_copy(
                tgt_basis.at[:, pl.ds(start, rows), :], tgt_tiles.at[:, half], load_sem.at[5 + half]
            )
        )
        loads.append(
            pltpu.make_async_copy(
                proj_basis.at[:, a * 2 + own], proj_tiles.at[:, half], load_sem.at[7 + half]
            )
        )
    for load in loads:
        load.start()

    barrier = pltpu.get_barrier_semaphore()
    pl.semaphore_signal(barrier, inc=1, device_id=core, device_id_type=pl.DeviceIdType.MESH)
    for delta in deltas[1:]:
        pl.semaphore_signal(
            barrier, inc=1, device_id=chip(delta), device_id_type=pl.DeviceIdType.MESH
        )

    for load in loads[:5]:
        load.wait()
    lane = lax.broadcasted_iota(jnp.int32, (1, points), 1)
    tile = 2 * r + lane // (points // 2)
    for d, delta in enumerate(deltas):
        at = chip(delta)
        live = jnp.logical_and(
            tile < counts[at["tgt"], at["prj"]], flags[at["tgt"], at["prj"]] > 0
        )
        masked[d] = jnp.where(live, weight[...], 0.0)
    for x in range(2):
        state[x, 0] = raw[x, 0].T

    pl.semaphore_wait(barrier, n)

    def remote(src, dst, send_sem, recv_sem, device):
        copy = pltpu.make_async_remote_copy(
            src_ref=src,
            dst_ref=dst,
            send_sem=send_sem,
            recv_sem=recv_sem,
            device_id=device,
            device_id_type=pl.DeviceIdType.MESH,
        )
        copy.start()
        return copy

    sent = []
    greet = []
    for x in range(2):
        greet.append(
            remote(raw.at[x, 0], raw.at[x, 1], init_send_sem.at[x], init_recv_sem.at[x], core)
        )
    for x in range(2):
        greet.append(
            remote(
                energy.at[x, 0], energy.at[x, 1], init_send_sem.at[2 + x], init_recv_sem.at[2 + x], core
            )
        )
    sent += greet
    tiles = (tgt_tiles, proj_tiles)
    grain = two_cols // n

    def project(rate, x, now):
        total = None
        for half in range(2):
            amp = now[half].astype(jnp.bfloat16)
            term = jnp.dot(
                amp, tiles[x][0, half], preferred_element_type=jnp.float32
            ) + jnp.dot(half_turn(amp), tiles[x][1, half], preferred_element_type=jnp.float32)
            total = term if total is None else total + term
        z_send[rate, x] = total.astype(jnp.bfloat16).reshape(n, grain, points)
        copies = []
        for d, delta in enumerate(deltas[1:]):
            copies.append(
                remote(
                    z_send.at[rate, x, chip_index(delta)],
                    z_recv.at[rate, x, d],
                    z_send_sem.at[rate, x, d],
                    z_recv_sem.at[rate, x, d],
                    chip(delta),
                )
            )
        sent.extend(copies)
        return copies

    def combine(rate, x, copies):
        for copy in copies:
            copy.wait_recv()

        def part(delta):
            d = deltas.index(delta)
            block = z_send[rate, x, me] if d == 0 else z_recv[rate, x, d - 1]
            return block.astype(jnp.float32)

        if x == 0:
            sums = [
                functools.reduce(jnp.add, [part((da, db)) for db in range(n_prj)])
                for da in range(n_tgt)
            ]
            fields = [
                functools.reduce(
                    jnp.add, [masked[deltas.index((da, eb))] * sums[da] for da in range(n_tgt)]
                )
                for eb in range(n_prj)
            ]
        else:
            sums = [
                functools.reduce(jnp.add, [part((da, db)) for da in range(n_tgt)])
                for db in range(n_prj)
            ]
            fields = [
                functools.reduce(
                    jnp.add, [masked[deltas.index((ea, db))] * sums[db] for db in range(n_prj)]
                )
                for ea in range(n_tgt)
            ]
        for e, field in enumerate(fields):
            f_send[rate, x, e] = field.astype(jnp.bfloat16)
        f_recv[rate, x, me] = fields[0].astype(jnp.bfloat16)
        replies = []
        for d, delta in enumerate(deltas[1:]):
            e = delta[1] if x == 0 else delta[0]
            replies.append(
                remote(
                    f_send.at[rate, x, e],
                    f_recv.at[rate, x, me],
                    f_send_sem.at[rate, x, d],
                    f_recv_sem.at[rate, x, d],
                    chip(delta),
                )
            )
        sent.extend(replies)
        return replies

    def expand_rows(rate, x, replies):
        for copy in replies:
            copy.wait_recv()
        other = tiles[1 - x]
        field = f_recv[rate, x].reshape(two_cols, points)
        turn = half_turn(field)
        contract = (((1,), (1,)), ((), ()))
        mine = []
        for half in (1, 0):
            term = lax.dot_general(
                field, other[0, half], contract, preferred_element_type=jnp.float32
            ) - lax.dot_general(turn, other[1, half], contract, preferred_element_type=jnp.float32)
            mine.insert(0, term)
            if half == 1 or rate == 0:
                y_send[rate, x, 1 - half] = term.astype(jnp.bfloat16)
        if rate == 0:
            copy = remote(
                y_send.at[0, x], y_recv.at[0, x], y_send_sem.at[0, x], y_recv_sem.at[0, x], core
            )
        else:
            copy = remote(
                y_send.at[1, x, 0], y_recv.at[1, x, 0], y_send_sem.at[1, x], y_recv_sem.at[1, x], core
            )
        sent.append(copy)
        return copy, mine

    def advance(rate, x, pending, half):
        _, mine = pending
        c = 1 - x
        total = mine[half] + y_recv[rate, x, half].astype(jnp.float32)
        amp = state[c, half]
        summed = energy[c, half] * (amp if rate == 0 else mid[c][0]) + total
        return amp + (0.5 * time_step if rate == 0 else time_step) * half_turn(summed)

    mid = [None, None]
    loads[5].wait()
    loads[7].wait()
    for copy in greet:
        copy.wait_recv()
    loads[6].wait()
    loads[8].wait()
    z = [None, None]
    for x in range(2):
        state[x, 1] = raw[x, 1].T
        z[x] = project(0, x, [state[x, 0], state[x, 1]])
    f = [combine(0, x, z[x]) for x in range(2)]
    y = [expand_rows(0, x, f[x]) for x in range(2)]
    for x in range(2):
        c = 1 - x
        y[x][0].wait_recv()
        mid[c] = [advance(0, x, y[x], half) for half in range(2)]
        z[c] = project(1, c, mid[c])
    f = [None, None]
    for x in (1, 0):
        f[x] = combine(1, x, z[x])
    y = [None, None]
    for x in (1, 0):
        y[x] = expand_rows(1, x, f[x])
    for x in (1, 0):
        y[x][0].wait_recv()
        new = advance(1, x, y[x], 0).T
        if x == 1:
            tgt_out[...] = new
        else:
            proj_out[0] = new
    for copy in sent:
        copy.wait_send()


def kernel_shards(
    n_tgt,
    n_prj,
    tgt_basis,
    proj_basis,
    quad_weight,
    tgt_energy,
    proj_energy,
    pair_flags,
    tile_counts,
    tgt_amp,
    proj_amp,
):
    n = n_tgt * n_prj
    rows, two_cols = tgt_amp.shape
    points = quad_weight.shape[0]
    grain = two_cols // n
    most = max(n_tgt, n_prj)
    hbm = pl.BlockSpec(memory_space=pltpu.HBM)
    smem = pl.BlockSpec(memory_space=pltpu.SMEM)
    vmem = pl.BlockSpec(memory_space=pltpu.VMEM)
    bf16, f32 = jnp.bfloat16, jnp.float32
    dma = pltpu.SemaphoreType.DMA
    return pl.pallas_call(
        functools.partial(step_kernel, n_tgt, n_prj),
        out_shape=(
            jax.ShapeDtypeStruct(tgt_amp.shape, f32),
            jax.ShapeDtypeStruct(proj_amp.shape, f32),
        ),
        in_specs=[hbm] * 5 + [smem] * 2 + [hbm] * 2,
        out_specs=(vmem, vmem),
        scratch_shapes=[
            pltpu.VMEM((2, 2, rows, points), bf16),
            pltpu.VMEM((2, 2, rows, points), bf16),
            pltpu.VMEM((1, points), f32),
            pltpu.VMEM((2, 2, 1, rows), f32),
            pltpu.VMEM((2, 2, rows, two_cols), f32),
            pltpu.VMEM((2, 2, two_cols, rows), f32),
            pltpu.VMEM((n, 1, points), f32),
            pltpu.VMEM((2, 2, n, grain, points), bf16),
            pltpu.VMEM((2, 2, n - 1, grain, points), bf16),
            pltpu.VMEM((2, 2, most, grain, points), bf16),
            pltpu.VMEM((2, 2, n, grain, points), bf16),
            pltpu.VMEM((2, 2, 2, two_cols, rows), bf16),
            pltpu.VMEM((2, 2, 2, two_cols, rows), bf16),
            dma((9,)),
            dma((4,)),
            dma((4,)),
            dma((2, 2, n - 1)),
            dma((2, 2, n - 1)),
            dma((2, 2, n - 1)),
            dma((2, 2, n - 1)),
            dma((2, 2)),
            dma((2, 2)),
        ],
        compiler_params=pltpu.CompilerParams(
            collective_id=0, has_side_effects=True, vmem_limit_bytes=32 * 1024 * 1024
        ),
    )(
        tgt_basis,
        proj_basis,
        quad_weight.reshape(1, points),
        tgt_energy.reshape(1, rows),
        proj_energy,
        pair_flags,
        tile_counts,
        tgt_amp,
        proj_amp,
    )


def power_of_two(value):
    return value & (value - 1) == 0


def solution(mesh):
    in_specs = (
        P(None, "tgt", "rep"),
        P(None, None, "prj", "rep"),
        P(("bpar", "rep")),
        P(("tgt", "prj", "rep")),
        P(("tgt", "rep"), "prj"),
        P("bpar", None),
        P("bpar", None),
        P(("bpar", "tgt", "prj", "rep"), None),
        P(("bpar", "tgt", "rep"), "prj", None),
    )
    out_specs = (P(("bpar", "tgt", "prj", "rep"), None), P(("bpar", "tgt", "rep"), "prj", None))
    n_tgt, n_prj = mesh.shape["tgt"], mesh.shape["prj"]
    if power_of_two(n_tgt) and power_of_two(n_prj) and n_tgt * n_prj <= 8:
        body = functools.partial(kernel_shards, n_tgt, n_prj)
    else:
        body = shards
    return jax.shard_map(body, mesh=mesh, in_specs=in_specs, out_specs=out_specs, check_vma=False)
```

```python
import functools

import jax
import jax.numpy as jnp
from jax import lax
from jax.experimental import pallas as pl
from jax.experimental.pallas import tpu as pltpu
from jax.sharding import PartitionSpec as P

time_step = 0.4


def rotate(energy, state_now, coupled):
    half_cols = state_now.shape[-1] // 2
    summed = energy[..., None] * state_now + coupled
    return jnp.concatenate([summed[..., half_cols:], -summed[..., :half_cols]], axis=-1)


def turned(amplitude):
    half_cols = amplitude.shape[-1] // 2
    return jnp.concatenate([amplitude[..., half_cols:], -amplitude[..., :half_cols]], axis=-1)


def conj_project(basis_real, basis_imag, amplitude):
    contract = (((0,), (0,)), ((), ()))
    first_part = lax.dot_general(
        basis_real, amplitude, contract, preferred_element_type=jnp.float32
    )
    second = lax.dot_general(
        basis_imag, turned(amplitude), contract, preferred_element_type=jnp.float32
    )
    return first_part + second


def expand(basis_real, basis_imag, projected):
    first_part = jnp.dot(basis_real, projected, preferred_element_type=jnp.float32)
    second = jnp.dot(basis_imag, turned(projected), preferred_element_type=jnp.float32)
    return first_part - second


def shards(
    tgt_basis,
    proj_basis,
    quad_weight,
    tgt_energy,
    proj_energy,
    pair_flags,
    tile_counts,
    tgt_amp,
    proj_amp,
):
    rep_index = lax.axis_index("rep")
    tgt_index = lax.axis_index("tgt")
    prj_index = lax.axis_index("prj")
    pair_flag = pair_flags[tgt_index, prj_index]
    pair_tiles = tile_counts[tgt_index, prj_index]
    tile_width = quad_weight.shape[0] // 2
    lower_tiles = (
        tgt_basis[..., :tile_width],
        proj_basis[..., :tile_width],
        quad_weight[:tile_width],
    )
    upper_tiles = (
        tgt_basis[..., tile_width:],
        proj_basis[..., tile_width:],
        quad_weight[tile_width:],
    )
    first_tiles = list(lower_tiles)
    second_tiles = list(upper_tiles)
    tile_ids = (2 * rep_index, 2 * rep_index + 1)
    slot_list = []
    for tile_id, tile_set in zip(tile_ids, (first_tiles, second_tiles)):
        is_live = jnp.logical_and(pair_flag > 0, tile_id < pair_tiles)
        slot_list.append((is_live, tile_set[0], tile_set[1], tile_set[2]))

    def coupled_rates(tgt_state, proj_state):
        tgt_send = tgt_state.astype(jnp.bfloat16)
        proj_send = proj_state.astype(jnp.bfloat16)
        two_cols = tgt_state.shape[-1]
        group_rows = proj_state.shape[1]
        zero_block = jnp.zeros((tile_width, two_cols), jnp.float32)
        shard_rows = lax.all_gather(tgt_send, ("prj", "rep"), axis=0, tiled=True)
        row_count = shard_rows.shape[0]
        updated = []
        for add_slot_index in range(2):
            is_live, tgt_tile = (slot_list[add_slot_index][0], slot_list[add_slot_index][1])
            basis_real = tgt_tile[0]
            basis_imag = tgt_tile[1]
            term = lax.cond(
                is_live,
                lambda: conj_project(basis_real, basis_imag, shard_rows),
                lambda: zero_block,
            )
            updated.append(term)
        tgt_raw = (updated[0], updated[1])
        target_coefficient = [
            (slot_list[slot_index][3][:, None] * tgt_raw[slot_index]).astype(jnp.bfloat16)
            for slot_index in range(2)
        ]

        def add_projectile(shard_rows):
            row_count = shard_rows.shape[0]
            flat_rows = shard_rows.reshape(row_count * group_rows, two_cols)
            updated = []
            for slot_index in range(2):
                is_live, proj_tile = (slot_list[slot_index][0], slot_list[slot_index][2])
                basis_real = proj_tile[0].reshape(row_count * group_rows, tile_width)
                basis_imag = proj_tile[1].reshape(row_count * group_rows, tile_width)
                term = lax.cond(
                    is_live,
                    lambda: conj_project(basis_real, basis_imag, flat_rows),
                    lambda: zero_block,
                )
                updated.append(term)
            return (updated[0], updated[1])

        proj_raw = add_projectile(lax.all_gather(proj_send, ("tgt", "rep"), axis=0, tiled=True))
        projectile_coefficient = [
            (slot_list[slot_index][3][:, None] * proj_raw[slot_index]).astype(jnp.bfloat16)
            for slot_index in range(2)
        ]
        row_count = proj_state.shape[0] * lax.axis_size(("tgt", "rep"))
        zero_terms = jnp.zeros((row_count, group_rows, two_cols), jnp.float32)
        summed = zero_terms
        for slot_index in range(2):
            is_live, proj_tile = (slot_list[slot_index][0], slot_list[slot_index][2])
            projectile_basis_real = proj_tile[0].reshape(row_count * group_rows, tile_width)
            projectile_basis_imag = proj_tile[1].reshape(row_count * group_rows, tile_width)
            coef_now = target_coefficient[slot_index]
            term = lax.cond(
                is_live,
                lambda: expand(projectile_basis_real, projectile_basis_imag, coef_now).reshape(
                    row_count, group_rows, two_cols
                ),
                lambda: zero_terms,
            )
            summed = summed + term
        proj_coupled = lax.psum_scatter(
            summed.astype(jnp.bfloat16), ("tgt", "rep"), scatter_dimension=0, tiled=True
        ).astype(jnp.float32)
        target_zero_terms = jnp.zeros(
            (tgt_state.shape[0] * lax.axis_size(("prj", "rep")), two_cols), jnp.float32
        )
        summed = target_zero_terms
        for slot_index in range(2):
            is_live, tgt_tile = (slot_list[slot_index][0], slot_list[slot_index][1])
            target_basis_real = tgt_tile[0]
            target_basis_imag = tgt_tile[1]
            target_coef_now = projectile_coefficient[slot_index]
            term = lax.cond(
                is_live,
                lambda: expand(target_basis_real, target_basis_imag, target_coef_now),
                lambda: target_zero_terms,
            )
            summed = summed + term
        tgt_coupled = lax.psum_scatter(
            summed.astype(jnp.bfloat16), ("prj", "rep"), scatter_dimension=0, tiled=True
        ).astype(jnp.float32)
        return (
            rotate(tgt_energy, tgt_state, tgt_coupled),
            rotate(proj_energy, proj_state, proj_coupled),
        )

    tgt_rate, proj_rate = coupled_rates(tgt_amp, proj_amp)
    tgt_half = tgt_amp + 0.5 * time_step * tgt_rate
    proj_half = proj_amp + 0.5 * time_step * proj_rate
    tgt_rate, proj_rate = coupled_rates(tgt_half, proj_half)
    return (tgt_amp + time_step * tgt_rate, proj_amp + time_step * proj_rate)


def half_turn(values):
    half = values.shape[0] // 2
    return jnp.concatenate([values[half:], -values[:half]], axis=0)


def step_kernel(
    n_tgt,
    n_prj,
    tgt_basis,
    proj_basis,
    quad_weight,
    tgt_energy,
    proj_energy,
    flags,
    counts,
    tgt_amp,
    proj_amp,
    tgt_out,
    proj_out,
    tgt_tiles,
    proj_tiles,
    weight,
    energy,
    raw,
    state,
    masked,
    z_send,
    z_recv,
    f_send,
    f_recv,
    y_send,
    y_recv,
    load_sem,
    init_send_sem,
    init_recv_sem,
    z_send_sem,
    z_recv_sem,
    f_send_sem,
    f_recv_sem,
    y_send_sem,
    y_recv_sem,
):
    n = n_tgt * n_prj
    a, b, r = lax.axis_index("tgt"), lax.axis_index("prj"), lax.axis_index("rep")
    me = a * n_prj + b
    rows = tgt_amp.shape[0]
    points = quad_weight.shape[1]
    two_cols = tgt_amp.shape[1]
    deltas = [(da, db) for da in range(n_tgt) for db in range(n_prj)]
    core = {"rep": 1 - r}

    def chip(delta):
        return {"tgt": lax.bitwise_xor(a, delta[0]), "prj": lax.bitwise_xor(b, delta[1])}

    def chip_index(delta):
        return lax.bitwise_xor(a, delta[0]) * n_prj + lax.bitwise_xor(b, delta[1])

    loads = [
        pltpu.make_async_copy(tgt_amp, raw.at[0, 0], load_sem.at[0]),
        pltpu.make_async_copy(proj_amp.at[0], raw.at[1, 0], load_sem.at[1]),
        pltpu.make_async_copy(tgt_energy, energy.at[0, 0], load_sem.at[2]),
        pltpu.make_async_copy(proj_energy, energy.at[1, 0], load_sem.at[3]),
        pltpu.make_async_copy(quad_weight, weight, load_sem.at[4]),
    ]
    for half in range(2):
        own = r if half == 0 else 1 - r
        start = pl.multiple_of((b * 2 + own) * rows, rows)
        loads.append(
            pltpu.make_async_copy(
                tgt_basis.at[:, pl.ds(start, rows), :], tgt_tiles.at[:, half], load_sem.at[5 + half]
            )
        )
        loads.append(
            pltpu.make_async_copy(
                proj_basis.at[:, a * 2 + own], proj_tiles.at[:, half], load_sem.at[7 + half]
            )
        )
    for load in loads:
        load.start()

    barrier = pltpu.get_barrier_semaphore()
    pl.semaphore_signal(barrier, inc=1, device_id=core, device_id_type=pl.DeviceIdType.MESH)
    for delta in deltas[1:]:
        pl.semaphore_signal(
            barrier, inc=1, device_id=chip(delta), device_id_type=pl.DeviceIdType.MESH
        )

    for load in loads[:5]:
        load.wait()
    lane = lax.broadcasted_iota(jnp.int32, (1, points), 1)
    tile = 2 * r + lane // (points // 2)
    for d, delta in enumerate(deltas):
        at = chip(delta)
        live = jnp.logical_and(
            tile < counts[at["prj"], at["tgt"]], flags[at["prj"], at["tgt"]] > 0
        )
        masked[d] = jnp.where(live, weight[...], 0.0)
    for x in range(2):
        state[x, 0] = raw[x, 0].T

    pl.semaphore_wait(barrier, n)

    def remote(src, dst, send_sem, recv_sem, device):
        copy = pltpu.make_async_remote_copy(
            src_ref=src,
            dst_ref=dst,
            send_sem=send_sem,
            recv_sem=recv_sem,
            device_id=device,
            device_id_type=pl.DeviceIdType.MESH,
        )
        copy.start()
        return copy

    sent = []
    greet = []
    for x in range(2):
        greet.append(
            remote(raw.at[x, 0], raw.at[x, 1], init_send_sem.at[x], init_recv_sem.at[x], core)
        )
    for x in range(2):
        greet.append(
            remote(
                energy.at[x, 0], energy.at[x, 1], init_send_sem.at[2 + x], init_recv_sem.at[2 + x], core
            )
        )
    sent += greet
    tiles = (tgt_tiles, proj_tiles)
    grain = two_cols // n

    def project(rate, x, now):
        total = None
        for half in range(2):
            amp = now[half].astype(jnp.bfloat16)
            term = jnp.dot(
                amp, tiles[x][0, half], preferred_element_type=jnp.float32
            ) + jnp.dot(half_turn(amp), tiles[x][1, half], preferred_element_type=jnp.float32)
            total = term if total is None else total + term
        z_send[rate, x] = total.astype(jnp.bfloat16).reshape(n, grain, points)
        copies = []
        for d, delta in enumerate(deltas[1:]):
            copies.append(
                remote(
                    z_send.at[rate, x, chip_index(delta)],
                    z_recv.at[rate, x, d],
                    z_send_sem.at[rate, x, d],
                    z_recv_sem.at[rate, x, d],
                    chip(delta),
                )
            )
        sent.extend(copies)
        return copies

    def combine(rate, x, copies):
        for copy in copies:
            copy.wait_recv()

        def part(delta):
            d = deltas.index(delta)
            block = z_send[rate, x, me] if d == 0 else z_recv[rate, x, d - 1]
            return block.astype(jnp.float32)

        if x == 0:
            sums = [
                functools.reduce(jnp.add, [part((da, db)) for db in range(n_prj)])
                for da in range(n_tgt)
            ]
            fields = [
                functools.reduce(
                    jnp.add, [masked[deltas.index((da, eb))] * sums[da] for da in range(n_tgt)]
                )
                for eb in range(n_prj)
            ]
        else:
            sums = [
                functools.reduce(jnp.add, [part((da, db)) for da in range(n_tgt)])
                for db in range(n_prj)
            ]
            fields = [
                functools.reduce(
                    jnp.add, [masked[deltas.index((ea, db))] * sums[db] for db in range(n_prj)]
                )
                for ea in range(n_tgt)
            ]
        for e, field in enumerate(fields):
            f_send[rate, x, e] = field.astype(jnp.bfloat16)
        f_recv[rate, x, me] = fields[0].astype(jnp.bfloat16)
        replies = []
        for d, delta in enumerate(deltas[1:]):
            e = delta[1] if x == 0 else delta[0]
            replies.append(
                remote(
                    f_send.at[rate, x, e],
                    f_recv.at[rate, x, me],
                    f_send_sem.at[rate, x, d],
                    f_recv_sem.at[rate, x, d],
                    chip(delta),
                )
            )
        sent.extend(replies)
        return replies

    def expand_rows(rate, x, replies):
        for copy in replies:
            copy.wait_recv()
        other = tiles[1 - x]
        field = f_recv[rate, x].reshape(two_cols, points)
        turn = half_turn(field)
        contract = (((1,), (1,)), ((), ()))
        mine = []
        for half in (1, 0):
            term = lax.dot_general(
                field, other[0, half], contract, preferred_element_type=jnp.float32
            ) - lax.dot_general(turn, other[1, half], contract, preferred_element_type=jnp.float32)
            mine.insert(0, term)
            if half == 1 or rate == 0:
                y_send[rate, x, 1 - half] = term.astype(jnp.bfloat16)
        if rate == 0:
            copy = remote(
                y_send.at[0, x], y_recv.at[0, x], y_send_sem.at[0, x], y_recv_sem.at[0, x], core
            )
        else:
            copy = remote(
                y_send.at[1, x, 0], y_recv.at[1, x, 0], y_send_sem.at[1, x], y_recv_sem.at[1, x], core
            )
        sent.append(copy)
        return copy, mine

    def advance(rate, x, pending, half):
        _, mine = pending
        c = 1 - x
        total = mine[half] + y_recv[rate, x, half].astype(jnp.float32)
        amp = state[c, half]
        summed = energy[c, half] * (amp if rate == 0 else mid[c][0]) + total
        return amp + (0.5 * time_step if rate == 0 else time_step) * half_turn(summed)

    mid = [None, None]
    loads[5].wait()
    loads[7].wait()
    for copy in greet:
        copy.wait_recv()
    loads[6].wait()
    loads[8].wait()
    z = [None, None]
    for x in range(2):
        state[x, 1] = raw[x, 1].T
        z[x] = project(0, x, [state[x, 0], state[x, 1]])
    f = [combine(0, x, z[x]) for x in range(2)]
    y = [expand_rows(0, x, f[x]) for x in range(2)]
    for x in range(2):
        c = 1 - x
        y[x][0].wait_recv()
        mid[c] = [advance(0, x, y[x], half) for half in range(2)]
        z[c] = project(1, c, mid[c])
    f = [None, None]
    for x in (1, 0):
        f[x] = combine(1, x, z[x])
    y = [None, None]
    for x in (1, 0):
        y[x] = expand_rows(1, x, f[x])
    for x in (1, 0):
        y[x][0].wait_recv()
        new = advance(1, x, y[x], 0).T
        if x == 1:
            tgt_out[...] = new
        else:
            proj_out[0] = new
    for copy in sent:
        copy.wait_send()


def kernel_shards(
    n_tgt,
    n_prj,
    tgt_basis,
    proj_basis,
    quad_weight,
    tgt_energy,
    proj_energy,
    pair_flags,
    tile_counts,
    tgt_amp,
    proj_amp,
):
    n = n_tgt * n_prj
    rows, two_cols = tgt_amp.shape
    points = quad_weight.shape[0]
    grain = two_cols // n
    most = max(n_tgt, n_prj)
    hbm = pl.BlockSpec(memory_space=pltpu.HBM)
    smem = pl.BlockSpec(memory_space=pltpu.SMEM)
    vmem = pl.BlockSpec(memory_space=pltpu.VMEM)
    bf16, f32 = jnp.bfloat16, jnp.float32
    dma = pltpu.SemaphoreType.DMA
    return pl.pallas_call(
        functools.partial(step_kernel, n_tgt, n_prj),
        out_shape=(
            jax.ShapeDtypeStruct(tgt_amp.shape, f32),
            jax.ShapeDtypeStruct(proj_amp.shape, f32),
        ),
        in_specs=[hbm] * 5 + [smem] * 2 + [hbm] * 2,
        out_specs=(vmem, vmem),
        scratch_shapes=[
            pltpu.VMEM((2, 2, rows, points), bf16),
            pltpu.VMEM((2, 2, rows, points), bf16),
            pltpu.VMEM((1, points), f32),
            pltpu.VMEM((2, 2, 1, rows), f32),
            pltpu.VMEM((2, 2, rows, two_cols), f32),
            pltpu.VMEM((2, 2, two_cols, rows), f32),
            pltpu.VMEM((n, 1, points), f32),
            pltpu.VMEM((2, 2, n, grain, points), bf16),
            pltpu.VMEM((2, 2, n - 1, grain, points), bf16),
            pltpu.VMEM((2, 2, most, grain, points), bf16),
            pltpu.VMEM((2, 2, n, grain, points), bf16),
            pltpu.VMEM((2, 2, 2, two_cols, rows), bf16),
            pltpu.VMEM((2, 2, 2, two_cols, rows), bf16),
            dma((9,)),
            dma((4,)),
            dma((4,)),
            dma((2, 2, n - 1)),
            dma((2, 2, n - 1)),
            dma((2, 2, n - 1)),
            dma((2, 2, n - 1)),
            dma((2, 2)),
            dma((2, 2)),
        ],
        compiler_params=pltpu.CompilerParams(
            collective_id=0, has_side_effects=True, vmem_limit_bytes=63 * 1024 * 1024
        ),
    )(
        tgt_basis,
        proj_basis,
        quad_weight.reshape(1, points),
        tgt_energy.reshape(1, rows),
        proj_energy,
        pair_flags.T,
        tile_counts.T,
        tgt_amp,
        proj_amp,
    )


def power_of_two(value):
    return value & (value - 1) == 0


def solution(mesh):
    in_specs = (
        P(None, "tgt", "rep"),
        P(None, None, "prj", "rep"),
        P(("bpar", "rep")),
        P(("tgt", "prj", "rep")),
        P(("tgt", "rep"), "prj"),
        P("bpar", None),
        P("bpar", None),
        P(("bpar", "tgt", "prj", "rep"), None),
        P(("bpar", "tgt", "rep"), "prj", None),
    )
    out_specs = (P(("bpar", "tgt", "prj", "rep"), None), P(("bpar", "tgt", "rep"), "prj", None))
    n_tgt, n_prj = mesh.shape["tgt"], mesh.shape["prj"]
    if power_of_two(n_tgt) and power_of_two(n_prj) and n_tgt * n_prj <= 8:
        body = functools.partial(kernel_shards, n_tgt, n_prj)
    else:
        body = shards
    return jax.shard_map(body, mesh=mesh, in_specs=in_specs, out_specs=out_specs, check_vma=False)
```

```python
import functools

import jax
import jax.numpy as jnp
from jax import lax
from jax.experimental import pallas as pl
from jax.experimental.pallas import tpu as pltpu
from jax.sharding import PartitionSpec as P

time_step = 0.4


def rotate(energy, state_now, coupled):
    half_cols = state_now.shape[-1] // 2
    summed = energy[..., None] * state_now + coupled
    return jnp.concatenate([summed[..., half_cols:], -summed[..., :half_cols]], axis=-1)


def turned(amplitude):
    half_cols = amplitude.shape[-1] // 2
    return jnp.concatenate([amplitude[..., half_cols:], -amplitude[..., :half_cols]], axis=-1)


def conj_project(basis_real, basis_imag, amplitude):
    contract = (((0,), (0,)), ((), ()))
    first_part = lax.dot_general(
        basis_real, amplitude, contract, preferred_element_type=jnp.float32
    )
    second = lax.dot_general(
        basis_imag, turned(amplitude), contract, preferred_element_type=jnp.float32
    )
    return first_part + second


def expand(basis_real, basis_imag, projected):
    first_part = jnp.dot(basis_real, projected, preferred_element_type=jnp.float32)
    second = jnp.dot(basis_imag, turned(projected), preferred_element_type=jnp.float32)
    return first_part - second


def shards(
    tgt_basis,
    proj_basis,
    quad_weight,
    tgt_energy,
    proj_energy,
    pair_flags,
    tile_counts,
    tgt_amp,
    proj_amp,
):
    rep_index = lax.axis_index("rep")
    tgt_index = lax.axis_index("tgt")
    prj_index = lax.axis_index("prj")
    pair_flag = pair_flags[tgt_index, prj_index]
    pair_tiles = tile_counts[tgt_index, prj_index]
    tile_width = quad_weight.shape[0] // 2
    lower_tiles = (
        tgt_basis[..., :tile_width],
        proj_basis[..., :tile_width],
        quad_weight[:tile_width],
    )
    upper_tiles = (
        tgt_basis[..., tile_width:],
        proj_basis[..., tile_width:],
        quad_weight[tile_width:],
    )
    first_tiles = list(lower_tiles)
    second_tiles = list(upper_tiles)
    tile_ids = (2 * rep_index, 2 * rep_index + 1)
    slot_list = []
    for tile_id, tile_set in zip(tile_ids, (first_tiles, second_tiles)):
        is_live = jnp.logical_and(pair_flag > 0, tile_id < pair_tiles)
        slot_list.append((is_live, tile_set[0], tile_set[1], tile_set[2]))

    def coupled_rates(tgt_state, proj_state):
        tgt_send = tgt_state.astype(jnp.bfloat16)
        proj_send = proj_state.astype(jnp.bfloat16)
        two_cols = tgt_state.shape[-1]
        group_rows = proj_state.shape[1]
        zero_block = jnp.zeros((tile_width, two_cols), jnp.float32)
        shard_rows = lax.all_gather(tgt_send, ("prj", "rep"), axis=0, tiled=True)
        row_count = shard_rows.shape[0]
        updated = []
        for add_slot_index in range(2):
            is_live, tgt_tile = (slot_list[add_slot_index][0], slot_list[add_slot_index][1])
            basis_real = tgt_tile[0]
            basis_imag = tgt_tile[1]
            term = lax.cond(
                is_live,
                lambda: conj_project(basis_real, basis_imag, shard_rows),
                lambda: zero_block,
            )
            updated.append(term)
        tgt_raw = (updated[0], updated[1])
        target_coefficient = [
            (slot_list[slot_index][3][:, None] * tgt_raw[slot_index]).astype(jnp.bfloat16)
            for slot_index in range(2)
        ]

        def add_projectile(shard_rows):
            row_count = shard_rows.shape[0]
            flat_rows = shard_rows.reshape(row_count * group_rows, two_cols)
            updated = []
            for slot_index in range(2):
                is_live, proj_tile = (slot_list[slot_index][0], slot_list[slot_index][2])
                basis_real = proj_tile[0].reshape(row_count * group_rows, tile_width)
                basis_imag = proj_tile[1].reshape(row_count * group_rows, tile_width)
                term = lax.cond(
                    is_live,
                    lambda: conj_project(basis_real, basis_imag, flat_rows),
                    lambda: zero_block,
                )
                updated.append(term)
            return (updated[0], updated[1])

        proj_raw = add_projectile(lax.all_gather(proj_send, ("tgt", "rep"), axis=0, tiled=True))
        projectile_coefficient = [
            (slot_list[slot_index][3][:, None] * proj_raw[slot_index]).astype(jnp.bfloat16)
            for slot_index in range(2)
        ]
        row_count = proj_state.shape[0] * lax.axis_size(("tgt", "rep"))
        zero_terms = jnp.zeros((row_count, group_rows, two_cols), jnp.float32)
        summed = zero_terms
        for slot_index in range(2):
            is_live, proj_tile = (slot_list[slot_index][0], slot_list[slot_index][2])
            projectile_basis_real = proj_tile[0].reshape(row_count * group_rows, tile_width)
            projectile_basis_imag = proj_tile[1].reshape(row_count * group_rows, tile_width)
            coef_now = target_coefficient[slot_index]
            term = lax.cond(
                is_live,
                lambda: expand(projectile_basis_real, projectile_basis_imag, coef_now).reshape(
                    row_count, group_rows, two_cols
                ),
                lambda: zero_terms,
            )
            summed = summed + term
        proj_coupled = lax.psum_scatter(
            summed.astype(jnp.bfloat16), ("tgt", "rep"), scatter_dimension=0, tiled=True
        ).astype(jnp.float32)
        target_zero_terms = jnp.zeros(
            (tgt_state.shape[0] * lax.axis_size(("prj", "rep")), two_cols), jnp.float32
        )
        summed = target_zero_terms
        for slot_index in range(2):
            is_live, tgt_tile = (slot_list[slot_index][0], slot_list[slot_index][1])
            target_basis_real = tgt_tile[0]
            target_basis_imag = tgt_tile[1]
            target_coef_now = projectile_coefficient[slot_index]
            term = lax.cond(
                is_live,
                lambda: expand(target_basis_real, target_basis_imag, target_coef_now),
                lambda: target_zero_terms,
            )
            summed = summed + term
        tgt_coupled = lax.psum_scatter(
            summed.astype(jnp.bfloat16), ("prj", "rep"), scatter_dimension=0, tiled=True
        ).astype(jnp.float32)
        return (
            rotate(tgt_energy, tgt_state, tgt_coupled),
            rotate(proj_energy, proj_state, proj_coupled),
        )

    tgt_rate, proj_rate = coupled_rates(tgt_amp, proj_amp)
    tgt_half = tgt_amp + 0.5 * time_step * tgt_rate
    proj_half = proj_amp + 0.5 * time_step * proj_rate
    tgt_rate, proj_rate = coupled_rates(tgt_half, proj_half)
    return (tgt_amp + time_step * tgt_rate, proj_amp + time_step * proj_rate)


def half_turn(values):
    half = values.shape[0] // 2
    return jnp.concatenate([values[half:], -values[:half]], axis=0)


def step_kernel(
    n_tgt,
    n_prj,
    tgt_basis,
    proj_basis,
    quad_weight,
    tgt_energy,
    proj_energy,
    flags,
    counts,
    tgt_amp,
    proj_amp,
    tgt_out,
    proj_out,
    tgt_tiles,
    proj_tiles,
    weight,
    energy,
    raw,
    state,
    masked,
    z_send,
    z_recv,
    f_send,
    f_recv,
    y_send,
    y_recv,
    load_sem,
    init_send_sem,
    init_recv_sem,
    z_send_sem,
    z_recv_sem,
    f_send_sem,
    f_recv_sem,
    y_send_sem,
    y_recv_sem,
):
    n = n_tgt * n_prj
    a, b, r = lax.axis_index("tgt"), lax.axis_index("prj"), lax.axis_index("rep")
    me = a * n_prj + b
    rows = tgt_amp.shape[0]
    points = quad_weight.shape[1]
    two_cols = tgt_amp.shape[1]
    deltas = [(da, db) for da in range(n_tgt) for db in range(n_prj)]
    core = {"rep": 1 - r}

    def chip(delta):
        return {"tgt": lax.bitwise_xor(a, delta[0]), "prj": lax.bitwise_xor(b, delta[1])}

    def chip_index(delta):
        return lax.bitwise_xor(a, delta[0]) * n_prj + lax.bitwise_xor(b, delta[1])

    loads = [
        pltpu.make_async_copy(tgt_amp, raw.at[0, 0], load_sem.at[0]),
        pltpu.make_async_copy(proj_amp.at[0], raw.at[1, 0], load_sem.at[1]),
        pltpu.make_async_copy(tgt_energy, energy.at[0, 0], load_sem.at[2]),
        pltpu.make_async_copy(proj_energy, energy.at[1, 0], load_sem.at[3]),
        pltpu.make_async_copy(quad_weight, weight, load_sem.at[4]),
    ]
    for half in range(2):
        own = r if half == 0 else 1 - r
        start = pl.multiple_of((b * 2 + own) * rows, rows)
        loads.append(
            pltpu.make_async_copy(
                tgt_basis.at[:, pl.ds(start, rows), :], tgt_tiles.at[:, half], load_sem.at[5 + half]
            )
        )
        loads.append(
            pltpu.make_async_copy(
                proj_basis.at[:, a * 2 + own], proj_tiles.at[:, half], load_sem.at[7 + half]
            )
        )
    for load in loads:
        load.start()

    barrier = pltpu.get_barrier_semaphore()
    pl.semaphore_signal(barrier, inc=1, device_id=core, device_id_type=pl.DeviceIdType.MESH)
    for delta in deltas[1:]:
        pl.semaphore_signal(
            barrier, inc=1, device_id=chip(delta), device_id_type=pl.DeviceIdType.MESH
        )

    for load in loads[:5]:
        load.wait()
    lane = lax.broadcasted_iota(jnp.int32, (1, points), 1)
    tile = 2 * r + lane // (points // 2)
    for d, delta in enumerate(deltas):
        at = chip(delta)
        live = jnp.logical_and(
            tile < counts[at["prj"], at["tgt"]], flags[at["prj"], at["tgt"]] > 0
        )
        masked[d] = jnp.where(live, weight[...], 0.0)
    for x in range(2):
        state[x, 0] = raw[x, 0].T

    pl.semaphore_wait(barrier, n)

    def remote(src, dst, send_sem, recv_sem, device):
        copy = pltpu.make_async_remote_copy(
            src_ref=src,
            dst_ref=dst,
            send_sem=send_sem,
            recv_sem=recv_sem,
            device_id=device,
            device_id_type=pl.DeviceIdType.MESH,
        )
        copy.start()
        return copy

    sent = []
    greet = []
    for x in range(2):
        greet.append(
            remote(raw.at[x, 0], raw.at[x, 1], init_send_sem.at[x], init_recv_sem.at[x], core)
        )
    for x in range(2):
        greet.append(
            remote(
                energy.at[x, 0], energy.at[x, 1], init_send_sem.at[2 + x], init_recv_sem.at[2 + x], core
            )
        )
    sent += greet
    tiles = (tgt_tiles, proj_tiles)
    grain = two_cols // n

    def project_half(x, half, now):
        amp = now.astype(jnp.bfloat16)
        return jnp.dot(amp, tiles[x][0, half], preferred_element_type=jnp.float32) + jnp.dot(
            half_turn(amp), tiles[x][1, half], preferred_element_type=jnp.float32
        )

    def spread(rate, x, total):
        z_send[rate, x] = total.astype(jnp.bfloat16).reshape(n, grain, points)
        copies = []
        for d, delta in reversed(list(enumerate(deltas[1:]))):
            copies.append(
                remote(
                    z_send.at[rate, x, chip_index(delta)],
                    z_recv.at[rate, x, d],
                    z_send_sem.at[rate, x, d],
                    z_recv_sem.at[rate, x, d],
                    chip(delta),
                )
            )
        sent.extend(copies)
        return copies

    def combine(rate, x, copies):
        for copy in copies:
            copy.wait_recv()

        def part(delta):
            d = deltas.index(delta)
            block = z_send[rate, x, me] if d == 0 else z_recv[rate, x, d - 1]
            return block.astype(jnp.float32)

        if x == 0:
            sums = [
                functools.reduce(jnp.add, [part((da, db)) for db in range(n_prj)])
                for da in range(n_tgt)
            ]
            fields = [
                functools.reduce(
                    jnp.add, [masked[deltas.index((da, eb))] * sums[da] for da in range(n_tgt)]
                )
                for eb in range(n_prj)
            ]
        else:
            sums = [
                functools.reduce(jnp.add, [part((da, db)) for da in range(n_tgt)])
                for db in range(n_prj)
            ]
            fields = [
                functools.reduce(
                    jnp.add, [masked[deltas.index((ea, db))] * sums[db] for db in range(n_prj)]
                )
                for ea in range(n_tgt)
            ]
        for e, field in enumerate(fields):
            f_send[rate, x, e] = field.astype(jnp.bfloat16)
        replies = []
        for d, delta in reversed(list(enumerate(deltas[1:]))):
            e = delta[1] if x == 0 else delta[0]
            replies.append(
                remote(
                    f_send.at[rate, x, e],
                    f_recv.at[rate, x, me],
                    f_send_sem.at[rate, x, d],
                    f_recv_sem.at[rate, x, d],
                    chip(delta),
                )
            )
        sent.extend(replies)
        f_recv[rate, x, me] = fields[0].astype(jnp.bfloat16)
        return replies

    def expand_rows(rate, x, replies):
        for copy in replies:
            copy.wait_recv()
        other = tiles[1 - x]
        field = f_recv[rate, x].reshape(two_cols, points)
        turn = half_turn(field)
        contract = (((1,), (1,)), ((), ()))
        mine = []
        for half in (1, 0):
            term = lax.dot_general(
                field, other[0, half], contract, preferred_element_type=jnp.float32
            ) - lax.dot_general(turn, other[1, half], contract, preferred_element_type=jnp.float32)
            mine.insert(0, term)
            if half == 1 or rate == 0:
                y_send[rate, x, 1 - half] = term.astype(jnp.bfloat16)
        if rate == 0:
            copy = remote(
                y_send.at[0, x], y_recv.at[0, x], y_send_sem.at[0, x], y_recv_sem.at[0, x], core
            )
        else:
            copy = remote(
                y_send.at[1, x, 0], y_recv.at[1, x, 0], y_send_sem.at[1, x], y_recv_sem.at[1, x], core
            )
        sent.append(copy)
        return copy, mine

    def advance(rate, x, pending, half):
        _, mine = pending
        c = 1 - x
        total = mine[half] + y_recv[rate, x, half].astype(jnp.float32)
        amp = state[c, half]
        summed = energy[c, half] * (amp if rate == 0 else mid[c][0]) + total
        return amp + (0.5 * time_step if rate == 0 else time_step) * half_turn(summed)

    mid = [None, None]
    z = [None, None]
    own = []
    for x in range(2):
        loads[5 + x].wait()
        own.append(project_half(x, 0, state[x, 0]))
    for x in range(2):
        loads[7 + x].wait()
        greet[x].wait_recv()
        state[x, 1] = raw[x, 1].T
        z[x] = spread(0, x, own[x] + project_half(x, 1, state[x, 1]))
    f = [combine(0, x, z[x]) for x in range(2)]
    y = [expand_rows(0, x, f[x]) for x in range(2)]
    for copy in greet[2:]:
        copy.wait_recv()
    for x in range(2):
        c = 1 - x
        y[x][0].wait_recv()
        mid[c] = [advance(0, x, y[x], half) for half in range(2)]
        z[c] = spread(1, c, project_half(c, 0, mid[c][0]) + project_half(c, 1, mid[c][1]))
    f = [None, None]
    for x in (1, 0):
        f[x] = combine(1, x, z[x])
    y = [None, None]
    for x in (1, 0):
        y[x] = expand_rows(1, x, f[x])
    for x in (1, 0):
        y[x][0].wait_recv()
        new = advance(1, x, y[x], 0).T
        if x == 1:
            tgt_out[...] = new
        else:
            proj_out[0] = new
    for copy in sent:
        copy.wait_send()


def kernel_shards(
    n_tgt,
    n_prj,
    tgt_basis,
    proj_basis,
    quad_weight,
    tgt_energy,
    proj_energy,
    pair_flags,
    tile_counts,
    tgt_amp,
    proj_amp,
):
    n = n_tgt * n_prj
    rows, two_cols = tgt_amp.shape
    points = quad_weight.shape[0]
    grain = two_cols // n
    most = max(n_tgt, n_prj)
    hbm = pl.BlockSpec(memory_space=pltpu.HBM)
    smem = pl.BlockSpec(memory_space=pltpu.SMEM)
    vmem = pl.BlockSpec(memory_space=pltpu.VMEM)
    bf16, f32 = jnp.bfloat16, jnp.float32
    dma = pltpu.SemaphoreType.DMA
    return pl.pallas_call(
        functools.partial(step_kernel, n_tgt, n_prj),
        out_shape=(
            pltpu.VMEM(tgt_amp.shape, f32),
            pltpu.VMEM(proj_amp.shape, f32),
        ),
        in_specs=[hbm] * 5 + [smem] * 2 + [hbm] * 2,
        out_specs=(vmem, vmem),
        scratch_shapes=[
            pltpu.VMEM((2, 2, rows, points), bf16),
            pltpu.VMEM((2, 2, rows, points), bf16),
            pltpu.VMEM((1, points), f32),
            pltpu.VMEM((2, 2, 1, rows), f32),
            pltpu.VMEM((2, 2, rows, two_cols), f32),
            pltpu.VMEM((2, 2, two_cols, rows), f32),
            pltpu.VMEM((n, 1, points), f32),
            pltpu.VMEM((2, 2, n, grain, points), bf16),
            pltpu.VMEM((2, 2, n - 1, grain, points), bf16),
            pltpu.VMEM((2, 2, most, grain, points), bf16),
            pltpu.VMEM((2, 2, n, grain, points), bf16),
            pltpu.VMEM((2, 2, 2, two_cols, rows), bf16),
            pltpu.VMEM((2, 2, 2, two_cols, rows), bf16),
            dma((9,)),
            dma((4,)),
            dma((4,)),
            dma((2, 2, n - 1)),
            dma((2, 2, n - 1)),
            dma((2, 2, n - 1)),
            dma((2, 2, n - 1)),
            dma((2, 2)),
            dma((2, 2)),
        ],
        compiler_params=pltpu.CompilerParams(
            collective_id=0, has_side_effects=True, vmem_limit_bytes=63 * 1024 * 1024
        ),
    )(
        tgt_basis,
        proj_basis,
        quad_weight.reshape(1, points),
        tgt_energy.reshape(1, rows),
        proj_energy,
        pair_flags.T,
        tile_counts.T,
        tgt_amp,
        proj_amp,
    )


def power_of_two(value):
    return value & (value - 1) == 0


def solution(mesh):
    in_specs = (
        P(None, "tgt", "rep"),
        P(None, None, "prj", "rep"),
        P(("bpar", "rep")),
        P(("tgt", "prj", "rep")),
        P(("tgt", "rep"), "prj"),
        P("bpar", None),
        P("bpar", None),
        P(("bpar", "tgt", "prj", "rep"), None),
        P(("bpar", "tgt", "rep"), "prj", None),
    )
    out_specs = (P(("bpar", "tgt", "prj", "rep"), None), P(("bpar", "tgt", "rep"), "prj", None))
    n_tgt, n_prj = mesh.shape["tgt"], mesh.shape["prj"]
    if power_of_two(n_tgt) and power_of_two(n_prj) and n_tgt * n_prj <= 8:
        body = functools.partial(kernel_shards, n_tgt, n_prj)
    else:
        body = shards
    return jax.shard_map(body, mesh=mesh, in_specs=in_specs, out_specs=out_specs, check_vma=False)
```

```python
import functools

import jax
import jax.numpy as jnp
from jax import lax
from jax.experimental import pallas as pl
from jax.experimental.pallas import tpu as pltpu
from jax.sharding import PartitionSpec as P

time_step = 0.4


def rotate(energy, state_now, coupled):
    half_cols = state_now.shape[-1] // 2
    summed = energy[..., None] * state_now + coupled
    return jnp.concatenate([summed[..., half_cols:], -summed[..., :half_cols]], axis=-1)


def turned(amplitude):
    half_cols = amplitude.shape[-1] // 2
    return jnp.concatenate([amplitude[..., half_cols:], -amplitude[..., :half_cols]], axis=-1)


def conj_project(basis_real, basis_imag, amplitude):
    contract = (((0,), (0,)), ((), ()))
    first_part = lax.dot_general(
        basis_real, amplitude, contract, preferred_element_type=jnp.float32
    )
    second = lax.dot_general(
        basis_imag, turned(amplitude), contract, preferred_element_type=jnp.float32
    )
    return first_part + second


def expand(basis_real, basis_imag, projected):
    first_part = jnp.dot(basis_real, projected, preferred_element_type=jnp.float32)
    second = jnp.dot(basis_imag, turned(projected), preferred_element_type=jnp.float32)
    return first_part - second


def shards(
    tgt_basis,
    proj_basis,
    quad_weight,
    tgt_energy,
    proj_energy,
    pair_flags,
    tile_counts,
    tgt_amp,
    proj_amp,
):
    rep_index = lax.axis_index("rep")
    tgt_index = lax.axis_index("tgt")
    prj_index = lax.axis_index("prj")
    pair_flag = pair_flags[tgt_index, prj_index]
    pair_tiles = tile_counts[tgt_index, prj_index]
    tile_width = quad_weight.shape[0] // 2
    lower_tiles = (
        tgt_basis[..., :tile_width],
        proj_basis[..., :tile_width],
        quad_weight[:tile_width],
    )
    upper_tiles = (
        tgt_basis[..., tile_width:],
        proj_basis[..., tile_width:],
        quad_weight[tile_width:],
    )
    first_tiles = list(lower_tiles)
    second_tiles = list(upper_tiles)
    tile_ids = (2 * rep_index, 2 * rep_index + 1)
    slot_list = []
    for tile_id, tile_set in zip(tile_ids, (first_tiles, second_tiles)):
        is_live = jnp.logical_and(pair_flag > 0, tile_id < pair_tiles)
        slot_list.append((is_live, tile_set[0], tile_set[1], tile_set[2]))

    def coupled_rates(tgt_state, proj_state):
        tgt_send = tgt_state.astype(jnp.bfloat16)
        proj_send = proj_state.astype(jnp.bfloat16)
        two_cols = tgt_state.shape[-1]
        group_rows = proj_state.shape[1]
        zero_block = jnp.zeros((tile_width, two_cols), jnp.float32)
        shard_rows = lax.all_gather(tgt_send, ("prj", "rep"), axis=0, tiled=True)
        row_count = shard_rows.shape[0]
        updated = []
        for add_slot_index in range(2):
            is_live, tgt_tile = (slot_list[add_slot_index][0], slot_list[add_slot_index][1])
            basis_real = tgt_tile[0]
            basis_imag = tgt_tile[1]
            term = lax.cond(
                is_live,
                lambda: conj_project(basis_real, basis_imag, shard_rows),
                lambda: zero_block,
            )
            updated.append(term)
        tgt_raw = (updated[0], updated[1])
        target_coefficient = [
            (slot_list[slot_index][3][:, None] * tgt_raw[slot_index]).astype(jnp.bfloat16)
            for slot_index in range(2)
        ]

        def add_projectile(shard_rows):
            row_count = shard_rows.shape[0]
            flat_rows = shard_rows.reshape(row_count * group_rows, two_cols)
            updated = []
            for slot_index in range(2):
                is_live, proj_tile = (slot_list[slot_index][0], slot_list[slot_index][2])
                basis_real = proj_tile[0].reshape(row_count * group_rows, tile_width)
                basis_imag = proj_tile[1].reshape(row_count * group_rows, tile_width)
                term = lax.cond(
                    is_live,
                    lambda: conj_project(basis_real, basis_imag, flat_rows),
                    lambda: zero_block,
                )
                updated.append(term)
            return (updated[0], updated[1])

        proj_raw = add_projectile(lax.all_gather(proj_send, ("tgt", "rep"), axis=0, tiled=True))
        projectile_coefficient = [
            (slot_list[slot_index][3][:, None] * proj_raw[slot_index]).astype(jnp.bfloat16)
            for slot_index in range(2)
        ]
        row_count = proj_state.shape[0] * lax.axis_size(("tgt", "rep"))
        zero_terms = jnp.zeros((row_count, group_rows, two_cols), jnp.float32)
        summed = zero_terms
        for slot_index in range(2):
            is_live, proj_tile = (slot_list[slot_index][0], slot_list[slot_index][2])
            projectile_basis_real = proj_tile[0].reshape(row_count * group_rows, tile_width)
            projectile_basis_imag = proj_tile[1].reshape(row_count * group_rows, tile_width)
            coef_now = target_coefficient[slot_index]
            term = lax.cond(
                is_live,
                lambda: expand(projectile_basis_real, projectile_basis_imag, coef_now).reshape(
                    row_count, group_rows, two_cols
                ),
                lambda: zero_terms,
            )
            summed = summed + term
        proj_coupled = lax.psum_scatter(
            summed.astype(jnp.bfloat16), ("tgt", "rep"), scatter_dimension=0, tiled=True
        ).astype(jnp.float32)
        target_zero_terms = jnp.zeros(
            (tgt_state.shape[0] * lax.axis_size(("prj", "rep")), two_cols), jnp.float32
        )
        summed = target_zero_terms
        for slot_index in range(2):
            is_live, tgt_tile = (slot_list[slot_index][0], slot_list[slot_index][1])
            target_basis_real = tgt_tile[0]
            target_basis_imag = tgt_tile[1]
            target_coef_now = projectile_coefficient[slot_index]
            term = lax.cond(
                is_live,
                lambda: expand(target_basis_real, target_basis_imag, target_coef_now),
                lambda: target_zero_terms,
            )
            summed = summed + term
        tgt_coupled = lax.psum_scatter(
            summed.astype(jnp.bfloat16), ("prj", "rep"), scatter_dimension=0, tiled=True
        ).astype(jnp.float32)
        return (
            rotate(tgt_energy, tgt_state, tgt_coupled),
            rotate(proj_energy, proj_state, proj_coupled),
        )

    tgt_rate, proj_rate = coupled_rates(tgt_amp, proj_amp)
    tgt_half = tgt_amp + 0.5 * time_step * tgt_rate
    proj_half = proj_amp + 0.5 * time_step * proj_rate
    tgt_rate, proj_rate = coupled_rates(tgt_half, proj_half)
    return (tgt_amp + time_step * tgt_rate, proj_amp + time_step * proj_rate)


def half_turn(values):
    half = values.shape[0] // 2
    return jnp.concatenate([values[half:], -values[:half]], axis=0)


def step_kernel(
    n_tgt,
    n_prj,
    tgt_basis,
    proj_basis,
    quad_weight,
    tgt_energy,
    proj_energy,
    flags,
    counts,
    tgt_amp,
    proj_amp,
    tgt_out,
    proj_out,
    tgt_tiles,
    proj_tiles,
    weight,
    energy,
    raw,
    state,
    masked,
    z_send,
    z_recv,
    f_send,
    f_recv,
    y_send,
    y_recv,
    load_sem,
    init_send_sem,
    init_recv_sem,
    z_send_sem,
    z_recv_sem,
    f_send_sem,
    f_recv_sem,
    y_send_sem,
    y_recv_sem,
):
    n = n_tgt * n_prj
    a, b, r = lax.axis_index("tgt"), lax.axis_index("prj"), lax.axis_index("rep")
    me = a * n_prj + b
    rows = tgt_amp.shape[0]
    points = quad_weight.shape[1]
    two_cols = tgt_amp.shape[1]
    deltas = [(da, db) for da in range(n_tgt) for db in range(n_prj)]
    core = {"rep": 1 - r}

    def chip(delta):
        return {"tgt": lax.bitwise_xor(a, delta[0]), "prj": lax.bitwise_xor(b, delta[1])}

    def chip_index(delta):
        return lax.bitwise_xor(a, delta[0]) * n_prj + lax.bitwise_xor(b, delta[1])

    loads = [
        pltpu.make_async_copy(tgt_amp, raw.at[0, 0], load_sem.at[0]),
        pltpu.make_async_copy(proj_amp.at[0], raw.at[1, 0], load_sem.at[1]),
        pltpu.make_async_copy(tgt_energy, energy.at[0, 0], load_sem.at[2]),
        pltpu.make_async_copy(proj_energy, energy.at[1, 0], load_sem.at[3]),
        pltpu.make_async_copy(quad_weight, weight, load_sem.at[4]),
    ]
    for half in range(2):
        own = r if half == 0 else 1 - r
        start = pl.multiple_of((b * 2 + own) * rows, rows)
        loads.append(
            pltpu.make_async_copy(
                tgt_basis.at[:, pl.ds(start, rows), :], tgt_tiles.at[:, half], load_sem.at[5 + half]
            )
        )
        loads.append(
            pltpu.make_async_copy(
                proj_basis.at[:, a * 2 + own], proj_tiles.at[:, half], load_sem.at[7 + half]
            )
        )
    for load in loads:
        load.start()

    barrier = pltpu.get_barrier_semaphore()
    pl.semaphore_signal(barrier, inc=1, device_id=core, device_id_type=pl.DeviceIdType.MESH)
    for delta in deltas[1:]:
        pl.semaphore_signal(
            barrier, inc=1, device_id=chip(delta), device_id_type=pl.DeviceIdType.MESH
        )

    for load in loads[:5]:
        load.wait()
    lane = lax.broadcasted_iota(jnp.int32, (1, points), 1)
    tile = 2 * r + lane // (points // 2)
    for d, delta in enumerate(deltas):
        at = chip(delta)
        live = jnp.logical_and(
            tile < counts[at["prj"], at["tgt"]], flags[at["prj"], at["tgt"]] > 0
        )
        masked[d] = jnp.where(live, weight[...], 0.0)
    for x in range(2):
        state[x, 0] = raw[x, 0].T

    pl.semaphore_wait(barrier, n)

    def remote(src, dst, send_sem, recv_sem, device):
        copy = pltpu.make_async_remote_copy(
            src_ref=src,
            dst_ref=dst,
            send_sem=send_sem,
            recv_sem=recv_sem,
            device_id=device,
            device_id_type=pl.DeviceIdType.MESH,
        )
        copy.start()
        return copy

    sent = []
    greet = []

    def settle(keep):
        while len(sent) > keep:
            sent.pop(0).wait_send()

    for x in range(2):
        greet.append(
            remote(raw.at[x, 0], raw.at[x, 1], init_send_sem.at[x], init_recv_sem.at[x], core)
        )
    for x in range(2):
        greet.append(
            remote(
                energy.at[x, 0], energy.at[x, 1], init_send_sem.at[2 + x], init_recv_sem.at[2 + x], core
            )
        )
    sent += greet
    tiles = (tgt_tiles, proj_tiles)
    grain = two_cols // n

    def project_half(x, half, now):
        amp = now.astype(jnp.bfloat16)
        return jnp.dot(amp, tiles[x][0, half], preferred_element_type=jnp.float32) + jnp.dot(
            half_turn(amp), tiles[x][1, half], preferred_element_type=jnp.float32
        )

    def spread(rate, x, total):
        z_send[rate, x] = total.astype(jnp.bfloat16).reshape(n, grain, points)
        copies = []
        for d, delta in reversed(list(enumerate(deltas[1:]))):
            copies.append(
                remote(
                    z_send.at[rate, x, chip_index(delta)],
                    z_recv.at[rate, x, d],
                    z_send_sem.at[rate, x, d],
                    z_recv_sem.at[rate, x, d],
                    chip(delta),
                )
            )
        sent.extend(copies)
        return copies

    def combine(rate, x, copies):
        for copy in copies:
            copy.wait_recv()

        def part(delta):
            d = deltas.index(delta)
            block = z_send[rate, x, me] if d == 0 else z_recv[rate, x, d - 1]
            return block.astype(jnp.float32)

        if x == 0:
            sums = [
                functools.reduce(jnp.add, [part((da, db)) for db in range(n_prj)])
                for da in range(n_tgt)
            ]
            fields = [
                functools.reduce(
                    jnp.add, [masked[deltas.index((da, eb))] * sums[da] for da in range(n_tgt)]
                )
                for eb in range(n_prj)
            ]
        else:
            sums = [
                functools.reduce(jnp.add, [part((da, db)) for da in range(n_tgt)])
                for db in range(n_prj)
            ]
            fields = [
                functools.reduce(
                    jnp.add, [masked[deltas.index((ea, db))] * sums[db] for db in range(n_prj)]
                )
                for ea in range(n_tgt)
            ]
        for e, field in enumerate(fields):
            f_send[rate, x, e] = field.astype(jnp.bfloat16)
        replies = []
        for d, delta in reversed(list(enumerate(deltas[1:]))):
            e = delta[1] if x == 0 else delta[0]
            replies.append(
                remote(
                    f_send.at[rate, x, e],
                    f_recv.at[rate, x, me],
                    f_send_sem.at[rate, x, d],
                    f_recv_sem.at[rate, x, d],
                    chip(delta),
                )
            )
        sent.extend(replies)
        f_recv[rate, x, me] = fields[0].astype(jnp.bfloat16)
        return replies

    def expand_rows(rate, x, replies):
        for copy in replies:
            copy.wait_recv()
        other = tiles[1 - x]
        field = f_recv[rate, x].reshape(two_cols, points)
        turn = half_turn(field)
        contract = (((1,), (1,)), ((), ()))
        mine = []
        for half in (1, 0):
            term = lax.dot_general(
                field, other[0, half], contract, preferred_element_type=jnp.float32
            ) - lax.dot_general(turn, other[1, half], contract, preferred_element_type=jnp.float32)
            mine.insert(0, term)
            if half == 1 or rate == 0:
                y_send[rate, x, 1 - half] = term.astype(jnp.bfloat16)
        if rate == 0:
            copy = remote(
                y_send.at[0, x], y_recv.at[0, x], y_send_sem.at[0, x], y_recv_sem.at[0, x], core
            )
        else:
            copy = remote(
                y_send.at[1, x, 0], y_recv.at[1, x, 0], y_send_sem.at[1, x], y_recv_sem.at[1, x], core
            )
        sent.append(copy)
        return copy, mine

    def advance(rate, x, pending, half):
        _, mine = pending
        c = 1 - x
        total = mine[half] + y_recv[rate, x, half].astype(jnp.float32)
        amp = state[c, half]
        summed = energy[c, half] * (amp if rate == 0 else mid[c][0]) + total
        return amp + (0.5 * time_step if rate == 0 else time_step) * half_turn(summed)

    mid = [None, None]
    z = [None, None]
    own = []
    for x in range(2):
        loads[5 + x].wait()
        own.append(project_half(x, 0, state[x, 0]))
    for x in range(2):
        loads[7 + x].wait()
        greet[x].wait_recv()
        state[x, 1] = raw[x, 1].T
        z[x] = spread(0, x, own[x] + project_half(x, 1, state[x, 1]))
    f = [combine(0, x, z[x]) for x in range(2)]
    y = [expand_rows(0, x, f[x]) for x in range(2)]
    for copy in greet[2:]:
        copy.wait_recv()
    settle(2 * (n - 1) + 2)
    for x in range(2):
        c = 1 - x
        y[x][0].wait_recv()
        mid[c] = [advance(0, x, y[x], half) for half in range(2)]
        z[c] = spread(1, c, project_half(c, 0, mid[c][0]) + project_half(c, 1, mid[c][1]))
    settle(2 * (n - 1))
    f = [None, None]
    for x in (1, 0):
        f[x] = combine(1, x, z[x])
    settle(2 * (n - 1))
    y = [None, None]
    for x in (1, 0):
        y[x] = expand_rows(1, x, f[x])
    settle(2)
    for x in (1, 0):
        y[x][0].wait_recv()
        new = advance(1, x, y[x], 0).T
        if x == 1:
            tgt_out[...] = new
        else:
            proj_out[0] = new
    settle(0)


def kernel_shards(
    n_tgt,
    n_prj,
    tgt_basis,
    proj_basis,
    quad_weight,
    tgt_energy,
    proj_energy,
    pair_flags,
    tile_counts,
    tgt_amp,
    proj_amp,
):
    n = n_tgt * n_prj
    rows, two_cols = tgt_amp.shape
    points = quad_weight.shape[0]
    grain = two_cols // n
    most = max(n_tgt, n_prj)
    hbm = pl.BlockSpec(memory_space=pltpu.HBM)
    smem = pl.BlockSpec(memory_space=pltpu.SMEM)
    vmem = pl.BlockSpec(memory_space=pltpu.VMEM)
    bf16, f32 = jnp.bfloat16, jnp.float32
    dma = pltpu.SemaphoreType.DMA
    return pl.pallas_call(
        functools.partial(step_kernel, n_tgt, n_prj),
        out_shape=(
            pltpu.VMEM(tgt_amp.shape, f32),
            pltpu.VMEM(proj_amp.shape, f32),
        ),
        in_specs=[hbm] * 5 + [smem] * 2 + [hbm] * 2,
        out_specs=(vmem, vmem),
        scratch_shapes=[
            pltpu.VMEM((2, 2, rows, points), bf16),
            pltpu.VMEM((2, 2, rows, points), bf16),
            pltpu.VMEM((1, points), f32),
            pltpu.VMEM((2, 2, 1, rows), f32),
            pltpu.VMEM((2, 2, rows, two_cols), f32),
            pltpu.VMEM((2, 2, two_cols, rows), f32),
            pltpu.VMEM((n, 1, points), f32),
            pltpu.VMEM((2, 2, n, grain, points), bf16),
            pltpu.VMEM((2, 2, n - 1, grain, points), bf16),
            pltpu.VMEM((2, 2, most, grain, points), bf16),
            pltpu.VMEM((2, 2, n, grain, points), bf16),
            pltpu.VMEM((2, 2, 2, two_cols, rows), bf16),
            pltpu.VMEM((2, 2, 2, two_cols, rows), bf16),
            dma((9,)),
            dma((4,)),
            dma((4,)),
            dma((2, 2, n - 1)),
            dma((2, 2, n - 1)),
            dma((2, 2, n - 1)),
            dma((2, 2, n - 1)),
            dma((2, 2)),
            dma((2, 2)),
        ],
        compiler_params=pltpu.CompilerParams(
            collective_id=0, has_side_effects=True, vmem_limit_bytes=63 * 1024 * 1024
        ),
    )(
        tgt_basis,
        proj_basis,
        quad_weight.reshape(1, points),
        tgt_energy.reshape(1, rows),
        proj_energy,
        pair_flags.T,
        tile_counts.T,
        tgt_amp,
        proj_amp,
    )


def power_of_two(value):
    return value & (value - 1) == 0


def solution(mesh):
    in_specs = (
        P(None, "tgt", "rep"),
        P(None, None, "prj", "rep"),
        P(("bpar", "rep")),
        P(("tgt", "prj", "rep")),
        P(("tgt", "rep"), "prj"),
        P("bpar", None),
        P("bpar", None),
        P(("bpar", "tgt", "prj", "rep"), None),
        P(("bpar", "tgt", "rep"), "prj", None),
    )
    out_specs = (P(("bpar", "tgt", "prj", "rep"), None), P(("bpar", "tgt", "rep"), "prj", None))
    n_tgt, n_prj = mesh.shape["tgt"], mesh.shape["prj"]
    if power_of_two(n_tgt) and power_of_two(n_prj) and n_tgt * n_prj <= 8:
        body = functools.partial(kernel_shards, n_tgt, n_prj)
    else:
        body = shards
    return jax.shard_map(body, mesh=mesh, in_specs=in_specs, out_specs=out_specs, check_vma=False)
```

```python
import functools

import jax
import jax.numpy as jnp
from jax import lax
from jax.experimental import pallas as pl
from jax.experimental.pallas import tpu as pltpu
from jax.sharding import PartitionSpec as P

time_step = 0.4


def rotate(energy, state_now, coupled):
    half_cols = state_now.shape[-1] // 2
    summed = energy[..., None] * state_now + coupled
    return jnp.concatenate([summed[..., half_cols:], -summed[..., :half_cols]], axis=-1)


def turned(amplitude):
    half_cols = amplitude.shape[-1] // 2
    return jnp.concatenate([amplitude[..., half_cols:], -amplitude[..., :half_cols]], axis=-1)


def conj_project(basis_real, basis_imag, amplitude):
    contract = (((0,), (0,)), ((), ()))
    first_part = lax.dot_general(
        basis_real, amplitude, contract, preferred_element_type=jnp.float32
    )
    second = lax.dot_general(
        basis_imag, turned(amplitude), contract, preferred_element_type=jnp.float32
    )
    return first_part + second


def expand(basis_real, basis_imag, projected):
    first_part = jnp.dot(basis_real, projected, preferred_element_type=jnp.float32)
    second = jnp.dot(basis_imag, turned(projected), preferred_element_type=jnp.float32)
    return first_part - second


def shards(
    tgt_basis,
    proj_basis,
    quad_weight,
    tgt_energy,
    proj_energy,
    pair_flags,
    tile_counts,
    tgt_amp,
    proj_amp,
):
    rep_index = lax.axis_index("rep")
    tgt_index = lax.axis_index("tgt")
    prj_index = lax.axis_index("prj")
    pair_flag = pair_flags[tgt_index, prj_index]
    pair_tiles = tile_counts[tgt_index, prj_index]
    tile_width = quad_weight.shape[0] // 2
    lower_tiles = (
        tgt_basis[..., :tile_width],
        proj_basis[..., :tile_width],
        quad_weight[:tile_width],
    )
    upper_tiles = (
        tgt_basis[..., tile_width:],
        proj_basis[..., tile_width:],
        quad_weight[tile_width:],
    )
    first_tiles = list(lower_tiles)
    second_tiles = list(upper_tiles)
    tile_ids = (2 * rep_index, 2 * rep_index + 1)
    slot_list = []
    for tile_id, tile_set in zip(tile_ids, (first_tiles, second_tiles)):
        is_live = jnp.logical_and(pair_flag > 0, tile_id < pair_tiles)
        slot_list.append((is_live, tile_set[0], tile_set[1], tile_set[2]))

    def coupled_rates(tgt_state, proj_state):
        tgt_send = tgt_state.astype(jnp.bfloat16)
        proj_send = proj_state.astype(jnp.bfloat16)
        two_cols = tgt_state.shape[-1]
        group_rows = proj_state.shape[1]
        zero_block = jnp.zeros((tile_width, two_cols), jnp.float32)
        shard_rows = lax.all_gather(tgt_send, ("prj", "rep"), axis=0, tiled=True)
        row_count = shard_rows.shape[0]
        updated = []
        for add_slot_index in range(2):
            is_live, tgt_tile = (slot_list[add_slot_index][0], slot_list[add_slot_index][1])
            basis_real = tgt_tile[0]
            basis_imag = tgt_tile[1]
            term = lax.cond(
                is_live,
                lambda: conj_project(basis_real, basis_imag, shard_rows),
                lambda: zero_block,
            )
            updated.append(term)
        tgt_raw = (updated[0], updated[1])
        target_coefficient = [
            (slot_list[slot_index][3][:, None] * tgt_raw[slot_index]).astype(jnp.bfloat16)
            for slot_index in range(2)
        ]

        def add_projectile(shard_rows):
            row_count = shard_rows.shape[0]
            flat_rows = shard_rows.reshape(row_count * group_rows, two_cols)
            updated = []
            for slot_index in range(2):
                is_live, proj_tile = (slot_list[slot_index][0], slot_list[slot_index][2])
                basis_real = proj_tile[0].reshape(row_count * group_rows, tile_width)
                basis_imag = proj_tile[1].reshape(row_count * group_rows, tile_width)
                term = lax.cond(
                    is_live,
                    lambda: conj_project(basis_real, basis_imag, flat_rows),
                    lambda: zero_block,
                )
                updated.append(term)
            return (updated[0], updated[1])

        proj_raw = add_projectile(lax.all_gather(proj_send, ("tgt", "rep"), axis=0, tiled=True))
        projectile_coefficient = [
            (slot_list[slot_index][3][:, None] * proj_raw[slot_index]).astype(jnp.bfloat16)
            for slot_index in range(2)
        ]
        row_count = proj_state.shape[0] * lax.axis_size(("tgt", "rep"))
        zero_terms = jnp.zeros((row_count, group_rows, two_cols), jnp.float32)
        summed = zero_terms
        for slot_index in range(2):
            is_live, proj_tile = (slot_list[slot_index][0], slot_list[slot_index][2])
            projectile_basis_real = proj_tile[0].reshape(row_count * group_rows, tile_width)
            projectile_basis_imag = proj_tile[1].reshape(row_count * group_rows, tile_width)
            coef_now = target_coefficient[slot_index]
            term = lax.cond(
                is_live,
                lambda: expand(projectile_basis_real, projectile_basis_imag, coef_now).reshape(
                    row_count, group_rows, two_cols
                ),
                lambda: zero_terms,
            )
            summed = summed + term
        proj_coupled = lax.psum_scatter(
            summed.astype(jnp.bfloat16), ("tgt", "rep"), scatter_dimension=0, tiled=True
        ).astype(jnp.float32)
        target_zero_terms = jnp.zeros(
            (tgt_state.shape[0] * lax.axis_size(("prj", "rep")), two_cols), jnp.float32
        )
        summed = target_zero_terms
        for slot_index in range(2):
            is_live, tgt_tile = (slot_list[slot_index][0], slot_list[slot_index][1])
            target_basis_real = tgt_tile[0]
            target_basis_imag = tgt_tile[1]
            target_coef_now = projectile_coefficient[slot_index]
            term = lax.cond(
                is_live,
                lambda: expand(target_basis_real, target_basis_imag, target_coef_now),
                lambda: target_zero_terms,
            )
            summed = summed + term
        tgt_coupled = lax.psum_scatter(
            summed.astype(jnp.bfloat16), ("prj", "rep"), scatter_dimension=0, tiled=True
        ).astype(jnp.float32)
        return (
            rotate(tgt_energy, tgt_state, tgt_coupled),
            rotate(proj_energy, proj_state, proj_coupled),
        )

    tgt_rate, proj_rate = coupled_rates(tgt_amp, proj_amp)
    tgt_half = tgt_amp + 0.5 * time_step * tgt_rate
    proj_half = proj_amp + 0.5 * time_step * proj_rate
    tgt_rate, proj_rate = coupled_rates(tgt_half, proj_half)
    return (tgt_amp + time_step * tgt_rate, proj_amp + time_step * proj_rate)


def half_turn(values):
    half = values.shape[0] // 2
    return jnp.concatenate([values[half:], -values[:half]], axis=0)


def step_kernel(
    n_tgt,
    n_prj,
    tgt_basis,
    proj_basis,
    quad_weight,
    tgt_energy,
    proj_energy,
    flags,
    counts,
    tgt_amp,
    proj_amp,
    tgt_out,
    proj_out,
    tgt_tiles,
    proj_tiles,
    weight,
    energy,
    raw,
    rounded,
    state,
    masked,
    z_send,
    z_recv,
    f_send,
    f_recv,
    y_send,
    y_recv,
    load_sem,
    init_send_sem,
    init_recv_sem,
    z_send_sem,
    z_recv_sem,
    f_send_sem,
    f_recv_sem,
    y_send_sem,
    y_recv_sem,
):
    n = n_tgt * n_prj
    a, b, r = lax.axis_index("tgt"), lax.axis_index("prj"), lax.axis_index("rep")
    me = a * n_prj + b
    rows = tgt_amp.shape[0]
    points = quad_weight.shape[1]
    two_cols = tgt_amp.shape[1]
    deltas = [(da, db) for da in range(n_tgt) for db in range(n_prj)]
    core = {"rep": 1 - r}

    def chip(delta):
        return {"tgt": lax.bitwise_xor(a, delta[0]), "prj": lax.bitwise_xor(b, delta[1])}

    def chip_index(delta):
        return lax.bitwise_xor(a, delta[0]) * n_prj + lax.bitwise_xor(b, delta[1])

    loads = [
        pltpu.make_async_copy(tgt_amp, raw.at[0, 0], load_sem.at[0]),
        pltpu.make_async_copy(proj_amp.at[0], raw.at[1, 0], load_sem.at[1]),
        pltpu.make_async_copy(tgt_energy, energy.at[0, 0], load_sem.at[2]),
        pltpu.make_async_copy(proj_energy, energy.at[1, 0], load_sem.at[3]),
        pltpu.make_async_copy(quad_weight, weight, load_sem.at[4]),
    ]
    for half in range(2):
        own = r if half == 0 else 1 - r
        start = pl.multiple_of((b * 2 + own) * rows, rows)
        loads.append(
            pltpu.make_async_copy(
                tgt_basis.at[:, pl.ds(start, rows), :], tgt_tiles.at[:, half], load_sem.at[5 + half]
            )
        )
        loads.append(
            pltpu.make_async_copy(
                proj_basis.at[:, a * 2 + own], proj_tiles.at[:, half], load_sem.at[7 + half]
            )
        )
    for load in loads:
        load.start()

    barrier = pltpu.get_barrier_semaphore()
    pl.semaphore_signal(barrier, inc=1, device_id=core, device_id_type=pl.DeviceIdType.MESH)
    for delta in deltas[1:]:
        pl.semaphore_signal(
            barrier, inc=1, device_id=chip(delta), device_id_type=pl.DeviceIdType.MESH
        )

    for load in loads[:5]:
        load.wait()
    lane = lax.broadcasted_iota(jnp.int32, (1, points), 1)
    tile = 2 * r + lane // (points // 2)
    for d, delta in enumerate(deltas):
        at = chip(delta)
        live = jnp.logical_and(
            tile < counts[at["prj"], at["tgt"]], flags[at["prj"], at["tgt"]] > 0
        )
        masked[d] = jnp.where(live, weight[...], 0.0)
    for x in range(2):
        state[x, 0] = raw[x, 0].T
        rounded[x, 0] = state[x, 0].astype(jnp.bfloat16)

    pl.semaphore_wait(barrier, n)

    def remote(src, dst, send_sem, recv_sem, device):
        copy = pltpu.make_async_remote_copy(
            src_ref=src,
            dst_ref=dst,
            send_sem=send_sem,
            recv_sem=recv_sem,
            device_id=device,
            device_id_type=pl.DeviceIdType.MESH,
        )
        copy.start()
        return copy

    sent = []
    greet = []

    def settle(keep):
        while len(sent) > keep:
            sent.pop(0).wait_send()

    early = [
        remote(
            rounded.at[x, 0], rounded.at[x, 1], init_send_sem.at[4 + x], init_recv_sem.at[4 + x], core
        )
        for x in range(2)
    ]
    sent += early
    for x in range(2):
        greet.append(
            remote(raw.at[x, 0], raw.at[x, 1], init_send_sem.at[x], init_recv_sem.at[x], core)
        )
    for x in range(2):
        greet.append(
            remote(
                energy.at[x, 0], energy.at[x, 1], init_send_sem.at[2 + x], init_recv_sem.at[2 + x], core
            )
        )
    sent += greet
    tiles = (tgt_tiles, proj_tiles)
    grain = two_cols // n

    def project_half(x, half, now):
        amp = now.astype(jnp.bfloat16)
        return jnp.dot(amp, tiles[x][0, half], preferred_element_type=jnp.float32) + jnp.dot(
            half_turn(amp), tiles[x][1, half], preferred_element_type=jnp.float32
        )

    def spread(rate, x, total):
        z_send[rate, x] = total.astype(jnp.bfloat16).reshape(n, grain, points)
        copies = []
        for d, delta in reversed(list(enumerate(deltas[1:]))):
            copies.append(
                remote(
                    z_send.at[rate, x, chip_index(delta)],
                    z_recv.at[rate, x, d],
                    z_send_sem.at[rate, x, d],
                    z_recv_sem.at[rate, x, d],
                    chip(delta),
                )
            )
        sent.extend(copies)
        return copies

    def combine(rate, x, copies):
        for copy in copies:
            copy.wait_recv()

        def part(delta):
            d = deltas.index(delta)
            block = z_send[rate, x, me] if d == 0 else z_recv[rate, x, d - 1]
            return block.astype(jnp.float32)

        if x == 0:
            sums = [
                functools.reduce(jnp.add, [part((da, db)) for db in range(n_prj)])
                for da in range(n_tgt)
            ]
            fields = [
                functools.reduce(
                    jnp.add, [masked[deltas.index((da, eb))] * sums[da] for da in range(n_tgt)]
                )
                for eb in range(n_prj)
            ]
        else:
            sums = [
                functools.reduce(jnp.add, [part((da, db)) for da in range(n_tgt)])
                for db in range(n_prj)
            ]
            fields = [
                functools.reduce(
                    jnp.add, [masked[deltas.index((ea, db))] * sums[db] for db in range(n_prj)]
                )
                for ea in range(n_tgt)
            ]
        for e, field in enumerate(fields):
            f_send[rate, x, e] = field.astype(jnp.bfloat16)
        replies = []
        for d, delta in reversed(list(enumerate(deltas[1:]))):
            e = delta[1] if x == 0 else delta[0]
            replies.append(
                remote(
                    f_send.at[rate, x, e],
                    f_recv.at[rate, x, me],
                    f_send_sem.at[rate, x, d],
                    f_recv_sem.at[rate, x, d],
                    chip(delta),
                )
            )
        sent.extend(replies)
        f_recv[rate, x, me] = fields[0].astype(jnp.bfloat16)
        return replies

    def expand_rows(rate, x, replies):
        for copy in replies:
            copy.wait_recv()
        other = tiles[1 - x]
        field = f_recv[rate, x].reshape(two_cols, points)
        turn = half_turn(field)
        contract = (((1,), (1,)), ((), ()))
        mine = []
        for half in (1, 0):
            term = lax.dot_general(
                field, other[0, half], contract, preferred_element_type=jnp.float32
            ) - lax.dot_general(turn, other[1, half], contract, preferred_element_type=jnp.float32)
            mine.insert(0, term)
            if half == 1 or rate == 0:
                y_send[rate, x, 1 - half] = term.astype(jnp.bfloat16)
        if rate == 0:
            copy = remote(
                y_send.at[0, x], y_recv.at[0, x], y_send_sem.at[0, x], y_recv_sem.at[0, x], core
            )
        else:
            copy = remote(
                y_send.at[1, x, 0], y_recv.at[1, x, 0], y_send_sem.at[1, x], y_recv_sem.at[1, x], core
            )
        sent.append(copy)
        return copy, mine

    def advance(rate, x, pending, half):
        _, mine = pending
        c = 1 - x
        total = mine[half] + y_recv[rate, x, half].astype(jnp.float32)
        amp = state[c, half]
        summed = energy[c, half] * (amp if rate == 0 else mid[c][0]) + total
        return amp + (0.5 * time_step if rate == 0 else time_step) * half_turn(summed)

    mid = [None, None]
    z = [None, None]
    own = []
    for x in range(2):
        loads[5 + x].wait()
        own.append(project_half(x, 0, rounded[x, 0]))
    for x in range(2):
        loads[7 + x].wait()
        early[x].wait_recv()
        z[x] = spread(0, x, own[x] + project_half(x, 1, rounded[x, 1]))
    for x in range(2):
        greet[x].wait_recv()
        state[x, 1] = raw[x, 1].T
    f = [combine(0, x, z[x]) for x in range(2)]
    y = [expand_rows(0, x, f[x]) for x in range(2)]
    for copy in greet[2:]:
        copy.wait_recv()
    settle(2 * (n - 1) + 2)
    for x in range(2):
        c = 1 - x
        y[x][0].wait_recv()
        mid[c] = [advance(0, x, y[x], half) for half in range(2)]
        z[c] = spread(1, c, project_half(c, 0, mid[c][0]) + project_half(c, 1, mid[c][1]))
    settle(2 * (n - 1))
    f = [None, None]
    for x in (1, 0):
        f[x] = combine(1, x, z[x])
    settle(2 * (n - 1))
    y = [None, None]
    for x in (1, 0):
        y[x] = expand_rows(1, x, f[x])
    settle(2)
    for x in (1, 0):
        y[x][0].wait_recv()
        new = advance(1, x, y[x], 0).T
        if x == 1:
            tgt_out[...] = new
        else:
            proj_out[0] = new
    settle(0)


def kernel_shards(
    n_tgt,
    n_prj,
    tgt_basis,
    proj_basis,
    quad_weight,
    tgt_energy,
    proj_energy,
    pair_flags,
    tile_counts,
    tgt_amp,
    proj_amp,
):
    n = n_tgt * n_prj
    rows, two_cols = tgt_amp.shape
    points = quad_weight.shape[0]
    grain = two_cols // n
    most = max(n_tgt, n_prj)
    hbm = pl.BlockSpec(memory_space=pltpu.HBM)
    smem = pl.BlockSpec(memory_space=pltpu.SMEM)
    vmem = pl.BlockSpec(memory_space=pltpu.VMEM)
    bf16, f32 = jnp.bfloat16, jnp.float32
    dma = pltpu.SemaphoreType.DMA
    return pl.pallas_call(
        functools.partial(step_kernel, n_tgt, n_prj),
        out_shape=(
            pltpu.VMEM(tgt_amp.shape, f32),
            pltpu.VMEM(proj_amp.shape, f32),
        ),
        in_specs=[hbm] * 5 + [smem] * 2 + [hbm] * 2,
        out_specs=(vmem, vmem),
        scratch_shapes=[
            pltpu.VMEM((2, 2, rows, points), bf16),
            pltpu.VMEM((2, 2, rows, points), bf16),
            pltpu.VMEM((1, points), f32),
            pltpu.VMEM((2, 2, 1, rows), f32),
            pltpu.VMEM((2, 2, rows, two_cols), f32),
            pltpu.VMEM((2, 2, two_cols, rows), bf16),
            pltpu.VMEM((2, 2, two_cols, rows), f32),
            pltpu.VMEM((n, 1, points), f32),
            pltpu.VMEM((2, 2, n, grain, points), bf16),
            pltpu.VMEM((2, 2, n - 1, grain, points), bf16),
            pltpu.VMEM((2, 2, most, grain, points), bf16),
            pltpu.VMEM((2, 2, n, grain, points), bf16),
            pltpu.VMEM((2, 2, 2, two_cols, rows), bf16),
            pltpu.VMEM((2, 2, 2, two_cols, rows), bf16),
            dma((9,)),
            dma((6,)),
            dma((6,)),
            dma((2, 2, n - 1)),
            dma((2, 2, n - 1)),
            dma((2, 2, n - 1)),
            dma((2, 2, n - 1)),
            dma((2, 2)),
            dma((2, 2)),
        ],
        compiler_params=pltpu.CompilerParams(
            collective_id=0, has_side_effects=True, vmem_limit_bytes=63 * 1024 * 1024
        ),
    )(
        tgt_basis,
        proj_basis,
        quad_weight.reshape(1, points),
        tgt_energy.reshape(1, rows),
        proj_energy,
        pair_flags.T,
        tile_counts.T,
        tgt_amp,
        proj_amp,
    )


def power_of_two(value):
    return value & (value - 1) == 0


def solution(mesh):
    in_specs = (
        P(None, "tgt", "rep"),
        P(None, None, "prj", "rep"),
        P(("bpar", "rep")),
        P(("tgt", "prj", "rep")),
        P(("tgt", "rep"), "prj"),
        P("bpar", None),
        P("bpar", None),
        P(("bpar", "tgt", "prj", "rep"), None),
        P(("bpar", "tgt", "rep"), "prj", None),
    )
    out_specs = (P(("bpar", "tgt", "prj", "rep"), None), P(("bpar", "tgt", "rep"), "prj", None))
    n_tgt, n_prj = mesh.shape["tgt"], mesh.shape["prj"]
    if power_of_two(n_tgt) and power_of_two(n_prj) and n_tgt * n_prj <= 8:
        body = functools.partial(kernel_shards, n_tgt, n_prj)
    else:
        body = shards
    return jax.shard_map(body, mesh=mesh, in_specs=in_specs, out_specs=out_specs, check_vma=False)
```

```python
import functools

import jax
import jax.numpy as jnp
from jax import lax
from jax.experimental import pallas as pl
from jax.experimental.pallas import tpu as pltpu
from jax.sharding import PartitionSpec as P

time_step = 0.4


def rotate(energy, state_now, coupled):
    half_cols = state_now.shape[-1] // 2
    summed = energy[..., None] * state_now + coupled
    return jnp.concatenate([summed[..., half_cols:], -summed[..., :half_cols]], axis=-1)


def turned(amplitude):
    half_cols = amplitude.shape[-1] // 2
    return jnp.concatenate([amplitude[..., half_cols:], -amplitude[..., :half_cols]], axis=-1)


def conj_project(basis_real, basis_imag, amplitude):
    contract = (((0,), (0,)), ((), ()))
    first_part = lax.dot_general(
        basis_real, amplitude, contract, preferred_element_type=jnp.float32
    )
    second = lax.dot_general(
        basis_imag, turned(amplitude), contract, preferred_element_type=jnp.float32
    )
    return first_part + second


def expand(basis_real, basis_imag, projected):
    first_part = jnp.dot(basis_real, projected, preferred_element_type=jnp.float32)
    second = jnp.dot(basis_imag, turned(projected), preferred_element_type=jnp.float32)
    return first_part - second


def shards(
    tgt_basis,
    proj_basis,
    quad_weight,
    tgt_energy,
    proj_energy,
    pair_flags,
    tile_counts,
    tgt_amp,
    proj_amp,
):
    rep_index = lax.axis_index("rep")
    tgt_index = lax.axis_index("tgt")
    prj_index = lax.axis_index("prj")
    pair_flag = pair_flags[tgt_index, prj_index]
    pair_tiles = tile_counts[tgt_index, prj_index]
    tile_width = quad_weight.shape[0] // 2
    lower_tiles = (
        tgt_basis[..., :tile_width],
        proj_basis[..., :tile_width],
        quad_weight[:tile_width],
    )
    upper_tiles = (
        tgt_basis[..., tile_width:],
        proj_basis[..., tile_width:],
        quad_weight[tile_width:],
    )
    first_tiles = list(lower_tiles)
    second_tiles = list(upper_tiles)
    tile_ids = (2 * rep_index, 2 * rep_index + 1)
    slot_list = []
    for tile_id, tile_set in zip(tile_ids, (first_tiles, second_tiles)):
        is_live = jnp.logical_and(pair_flag > 0, tile_id < pair_tiles)
        slot_list.append((is_live, tile_set[0], tile_set[1], tile_set[2]))

    def coupled_rates(tgt_state, proj_state):
        tgt_send = tgt_state.astype(jnp.bfloat16)
        proj_send = proj_state.astype(jnp.bfloat16)
        two_cols = tgt_state.shape[-1]
        group_rows = proj_state.shape[1]
        zero_block = jnp.zeros((tile_width, two_cols), jnp.float32)
        shard_rows = lax.all_gather(tgt_send, ("prj", "rep"), axis=0, tiled=True)
        row_count = shard_rows.shape[0]
        updated = []
        for add_slot_index in range(2):
            is_live, tgt_tile = (slot_list[add_slot_index][0], slot_list[add_slot_index][1])
            basis_real = tgt_tile[0]
            basis_imag = tgt_tile[1]
            term = lax.cond(
                is_live,
                lambda: conj_project(basis_real, basis_imag, shard_rows),
                lambda: zero_block,
            )
            updated.append(term)
        tgt_raw = (updated[0], updated[1])
        target_coefficient = [
            (slot_list[slot_index][3][:, None] * tgt_raw[slot_index]).astype(jnp.bfloat16)
            for slot_index in range(2)
        ]

        def add_projectile(shard_rows):
            row_count = shard_rows.shape[0]
            flat_rows = shard_rows.reshape(row_count * group_rows, two_cols)
            updated = []
            for slot_index in range(2):
                is_live, proj_tile = (slot_list[slot_index][0], slot_list[slot_index][2])
                basis_real = proj_tile[0].reshape(row_count * group_rows, tile_width)
                basis_imag = proj_tile[1].reshape(row_count * group_rows, tile_width)
                term = lax.cond(
                    is_live,
                    lambda: conj_project(basis_real, basis_imag, flat_rows),
                    lambda: zero_block,
                )
                updated.append(term)
            return (updated[0], updated[1])

        proj_raw = add_projectile(lax.all_gather(proj_send, ("tgt", "rep"), axis=0, tiled=True))
        projectile_coefficient = [
            (slot_list[slot_index][3][:, None] * proj_raw[slot_index]).astype(jnp.bfloat16)
            for slot_index in range(2)
        ]
        row_count = proj_state.shape[0] * lax.axis_size(("tgt", "rep"))
        zero_terms = jnp.zeros((row_count, group_rows, two_cols), jnp.float32)
        summed = zero_terms
        for slot_index in range(2):
            is_live, proj_tile = (slot_list[slot_index][0], slot_list[slot_index][2])
            projectile_basis_real = proj_tile[0].reshape(row_count * group_rows, tile_width)
            projectile_basis_imag = proj_tile[1].reshape(row_count * group_rows, tile_width)
            coef_now = target_coefficient[slot_index]
            term = lax.cond(
                is_live,
                lambda: expand(projectile_basis_real, projectile_basis_imag, coef_now).reshape(
                    row_count, group_rows, two_cols
                ),
                lambda: zero_terms,
            )
            summed = summed + term
        proj_coupled = lax.psum_scatter(
            summed.astype(jnp.bfloat16), ("tgt", "rep"), scatter_dimension=0, tiled=True
        ).astype(jnp.float32)
        target_zero_terms = jnp.zeros(
            (tgt_state.shape[0] * lax.axis_size(("prj", "rep")), two_cols), jnp.float32
        )
        summed = target_zero_terms
        for slot_index in range(2):
            is_live, tgt_tile = (slot_list[slot_index][0], slot_list[slot_index][1])
            target_basis_real = tgt_tile[0]
            target_basis_imag = tgt_tile[1]
            target_coef_now = projectile_coefficient[slot_index]
            term = lax.cond(
                is_live,
                lambda: expand(target_basis_real, target_basis_imag, target_coef_now),
                lambda: target_zero_terms,
            )
            summed = summed + term
        tgt_coupled = lax.psum_scatter(
            summed.astype(jnp.bfloat16), ("prj", "rep"), scatter_dimension=0, tiled=True
        ).astype(jnp.float32)
        return (
            rotate(tgt_energy, tgt_state, tgt_coupled),
            rotate(proj_energy, proj_state, proj_coupled),
        )

    tgt_rate, proj_rate = coupled_rates(tgt_amp, proj_amp)
    tgt_half = tgt_amp + 0.5 * time_step * tgt_rate
    proj_half = proj_amp + 0.5 * time_step * proj_rate
    tgt_rate, proj_rate = coupled_rates(tgt_half, proj_half)
    return (tgt_amp + time_step * tgt_rate, proj_amp + time_step * proj_rate)


def half_turn(values):
    half = values.shape[0] // 2
    return jnp.concatenate([values[half:], -values[:half]], axis=0)


def step_kernel(
    n_tgt,
    n_prj,
    tgt_basis,
    proj_basis,
    quad_weight,
    tgt_energy,
    proj_energy,
    flags,
    counts,
    tgt_amp,
    proj_amp,
    tgt_out,
    proj_out,
    tgt_tiles,
    proj_tiles,
    weight,
    energy,
    raw,
    rounded,
    state,
    masked,
    z_send,
    z_recv,
    f_send,
    f_recv,
    y_send,
    y_recv,
    load_sem,
    init_send_sem,
    init_recv_sem,
    z_send_sem,
    z_recv_sem,
    f_send_sem,
    f_recv_sem,
    y_send_sem,
    y_recv_sem,
):
    n = n_tgt * n_prj
    a, b, r = lax.axis_index("tgt"), lax.axis_index("prj"), lax.axis_index("rep")
    me = a * n_prj + b
    rows = tgt_amp.shape[0]
    points = quad_weight.shape[1]
    two_cols = tgt_amp.shape[1]
    deltas = [(da, db) for da in range(n_tgt) for db in range(n_prj)]
    core = {"rep": 1 - r}

    def chip(delta):
        return {"tgt": lax.bitwise_xor(a, delta[0]), "prj": lax.bitwise_xor(b, delta[1])}

    def chip_index(delta):
        return lax.bitwise_xor(a, delta[0]) * n_prj + lax.bitwise_xor(b, delta[1])

    loads = [
        pltpu.make_async_copy(tgt_amp, raw.at[0, 0], load_sem.at[0]),
        pltpu.make_async_copy(proj_amp.at[0], raw.at[1, 0], load_sem.at[1]),
        pltpu.make_async_copy(tgt_energy, energy.at[0, 0], load_sem.at[2]),
        pltpu.make_async_copy(proj_energy, energy.at[1, 0], load_sem.at[3]),
        pltpu.make_async_copy(quad_weight, weight, load_sem.at[4]),
    ]
    for half in range(2):
        own = r if half == 0 else 1 - r
        start = pl.multiple_of((b * 2 + own) * rows, rows)
        loads.append(
            pltpu.make_async_copy(
                tgt_basis.at[:, pl.ds(start, rows), :], tgt_tiles.at[:, half], load_sem.at[5 + half]
            )
        )
        loads.append(
            pltpu.make_async_copy(
                proj_basis.at[:, a * 2 + own], proj_tiles.at[:, half], load_sem.at[7 + half]
            )
        )
    for load in loads:
        load.start()

    barrier = pltpu.get_barrier_semaphore()
    pl.semaphore_signal(barrier, inc=1, device_id=core, device_id_type=pl.DeviceIdType.MESH)
    for delta in deltas[1:]:
        pl.semaphore_signal(
            barrier, inc=1, device_id=chip(delta), device_id_type=pl.DeviceIdType.MESH
        )

    for load in loads[:5]:
        load.wait()
    lane = lax.broadcasted_iota(jnp.int32, (1, points), 1)
    tile = 2 * r + lane // (points // 2)
    for d, delta in enumerate(deltas):
        at = chip(delta)
        live = jnp.logical_and(
            tile < counts[at["prj"], at["tgt"]], flags[at["prj"], at["tgt"]] > 0
        )
        masked[d] = jnp.where(live, weight[...], 0.0)
    for x in range(2):
        state[x, 0] = raw[x, 0].T
        rounded[x, 0] = state[x, 0].astype(jnp.bfloat16)

    pl.semaphore_wait(barrier, n)

    def remote(src, dst, send_sem, recv_sem, device):
        copy = pltpu.make_async_remote_copy(
            src_ref=src,
            dst_ref=dst,
            send_sem=send_sem,
            recv_sem=recv_sem,
            device_id=device,
            device_id_type=pl.DeviceIdType.MESH,
        )
        copy.start()
        return copy

    sent = []
    greet = []

    def settle(keep):
        while len(sent) > keep:
            sent.pop(0).wait_send()

    early = [
        remote(
            rounded.at[x, 0], rounded.at[x, 1], init_send_sem.at[4 + x], init_recv_sem.at[4 + x], core
        )
        for x in range(2)
    ]
    sent += early
    for x in range(2):
        greet.append(
            remote(raw.at[x, 0], raw.at[x, 1], init_send_sem.at[x], init_recv_sem.at[x], core)
        )
    for x in range(2):
        greet.append(
            remote(
                energy.at[x, 0], energy.at[x, 1], init_send_sem.at[2 + x], init_recv_sem.at[2 + x], core
            )
        )
    sent += greet
    tiles = (tgt_tiles, proj_tiles)
    grain = two_cols // n

    def project_half(x, half, now):
        amp = now.astype(jnp.bfloat16)
        return jnp.dot(amp, tiles[x][0, half], preferred_element_type=jnp.float32) + jnp.dot(
            half_turn(amp), tiles[x][1, half], preferred_element_type=jnp.float32
        )

    def spread(rate, x, total):
        z_send[rate, x] = total.astype(jnp.bfloat16).reshape(n, grain, points)
        copies = []
        for d, delta in reversed(list(enumerate(deltas[1:]))):
            copies.append(
                remote(
                    z_send.at[rate, x, chip_index(delta)],
                    z_recv.at[rate, x, d],
                    z_send_sem.at[rate, x, d],
                    z_recv_sem.at[rate, x],
                    chip(delta),
                )
            )
        sent.extend(copies)
        return copies

    def combine(rate, x, copies):
        pltpu.make_async_copy(
            z_recv.at[rate, x], z_recv.at[rate, x], z_recv_sem.at[rate, x]
        ).wait()

        def part(delta):
            d = deltas.index(delta)
            block = z_send[rate, x, me] if d == 0 else z_recv[rate, x, d - 1]
            return block.astype(jnp.float32)

        if x == 0:
            sums = [
                functools.reduce(jnp.add, [part((da, db)) for db in range(n_prj)])
                for da in range(n_tgt)
            ]
            fields = [
                functools.reduce(
                    jnp.add, [masked[deltas.index((da, eb))] * sums[da] for da in range(n_tgt)]
                )
                for eb in range(n_prj)
            ]
        else:
            sums = [
                functools.reduce(jnp.add, [part((da, db)) for da in range(n_tgt)])
                for db in range(n_prj)
            ]
            fields = [
                functools.reduce(
                    jnp.add, [masked[deltas.index((ea, db))] * sums[db] for db in range(n_prj)]
                )
                for ea in range(n_tgt)
            ]
        for e, field in enumerate(fields):
            f_send[rate, x, e] = field.astype(jnp.bfloat16)
        replies = []
        for d, delta in reversed(list(enumerate(deltas[1:]))):
            e = delta[1] if x == 0 else delta[0]
            replies.append(
                remote(
                    f_send.at[rate, x, e],
                    f_recv.at[rate, x, me],
                    f_send_sem.at[rate, x, d],
                    f_recv_sem.at[rate, x],
                    chip(delta),
                )
            )
        sent.extend(replies)
        f_recv[rate, x, me] = fields[0].astype(jnp.bfloat16)
        return replies

    def expand_rows(rate, x, replies):
        landed = f_recv.at[rate, x, pl.ds(0, n - 1)]
        pltpu.make_async_copy(landed, landed, f_recv_sem.at[rate, x]).wait()
        other = tiles[1 - x]
        field = f_recv[rate, x].reshape(two_cols, points)
        turn = half_turn(field)
        contract = (((1,), (1,)), ((), ()))
        mine = []
        for half in (1, 0):
            term = lax.dot_general(
                field, other[0, half], contract, preferred_element_type=jnp.float32
            ) - lax.dot_general(turn, other[1, half], contract, preferred_element_type=jnp.float32)
            mine.insert(0, term)
            if half == 1 or rate == 0:
                y_send[rate, x, 1 - half] = term.astype(jnp.bfloat16)
        if rate == 0:
            copy = remote(
                y_send.at[0, x], y_recv.at[0, x], y_send_sem.at[0, x], y_recv_sem.at[0, x], core
            )
        else:
            copy = remote(
                y_send.at[1, x, 0], y_recv.at[1, x, 0], y_send_sem.at[1, x], y_recv_sem.at[1, x], core
            )
        sent.append(copy)
        return copy, mine

    def advance(rate, x, pending, half):
        _, mine = pending
        c = 1 - x
        total = mine[half] + y_recv[rate, x, half].astype(jnp.float32)
        amp = state[c, half]
        summed = energy[c, half] * (amp if rate == 0 else mid[c][0]) + total
        return amp + (0.5 * time_step if rate == 0 else time_step) * half_turn(summed)

    mid = [None, None]
    z = [None, None]
    own = []
    for x in range(2):
        loads[5 + x].wait()
        own.append(project_half(x, 0, rounded[x, 0]))
    for x in range(2):
        loads[7 + x].wait()
        early[x].wait_recv()
        z[x] = spread(0, x, own[x] + project_half(x, 1, rounded[x, 1]))
    for x in range(2):
        greet[x].wait_recv()
        state[x, 1] = raw[x, 1].T
    f = [combine(0, x, z[x]) for x in range(2)]
    y = [expand_rows(0, x, f[x]) for x in range(2)]
    for copy in greet[2:]:
        copy.wait_recv()
    settle(2 * (n - 1) + 2)
    for x in range(2):
        c = 1 - x
        y[x][0].wait_recv()
        mid[c] = [advance(0, x, y[x], half) for half in range(2)]
        z[c] = spread(1, c, project_half(c, 0, mid[c][0]) + project_half(c, 1, mid[c][1]))
    settle(2 * (n - 1))
    f = [None, None]
    for x in (1, 0):
        f[x] = combine(1, x, z[x])
    y = [None, None]
    for x in (1, 0):
        y[x] = expand_rows(1, x, f[x])
    settle(2)
    for x in (1, 0):
        y[x][0].wait_recv()
        new = advance(1, x, y[x], 0).T
        if x == 1:
            tgt_out[...] = new
        else:
            proj_out[0] = new
    settle(0)


def kernel_shards(
    n_tgt,
    n_prj,
    tgt_basis,
    proj_basis,
    quad_weight,
    tgt_energy,
    proj_energy,
    pair_flags,
    tile_counts,
    tgt_amp,
    proj_amp,
):
    n = n_tgt * n_prj
    rows, two_cols = tgt_amp.shape
    points = quad_weight.shape[0]
    grain = two_cols // n
    most = max(n_tgt, n_prj)
    hbm = pl.BlockSpec(memory_space=pltpu.HBM)
    smem = pl.BlockSpec(memory_space=pltpu.SMEM)
    vmem = pl.BlockSpec(memory_space=pltpu.VMEM)
    bf16, f32 = jnp.bfloat16, jnp.float32
    dma = pltpu.SemaphoreType.DMA
    return pl.pallas_call(
        functools.partial(step_kernel, n_tgt, n_prj),
        out_shape=(
            pltpu.VMEM(tgt_amp.shape, f32),
            pltpu.VMEM(proj_amp.shape, f32),
        ),
        in_specs=[hbm] * 5 + [smem] * 2 + [hbm] * 2,
        out_specs=(vmem, vmem),
        scratch_shapes=[
            pltpu.VMEM((2, 2, rows, points), bf16),
            pltpu.VMEM((2, 2, rows, points), bf16),
            pltpu.VMEM((1, points), f32),
            pltpu.VMEM((2, 2, 1, rows), f32),
            pltpu.VMEM((2, 2, rows, two_cols), f32),
            pltpu.VMEM((2, 2, two_cols, rows), bf16),
            pltpu.VMEM((2, 2, two_cols, rows), f32),
            pltpu.VMEM((n, 1, points), f32),
            pltpu.VMEM((2, 2, n, grain, points), bf16),
            pltpu.VMEM((2, 2, n - 1, grain, points), bf16),
            pltpu.VMEM((2, 2, most, grain, points), bf16),
            pltpu.VMEM((2, 2, n, grain, points), bf16),
            pltpu.VMEM((2, 2, 2, two_cols, rows), bf16),
            pltpu.VMEM((2, 2, 2, two_cols, rows), bf16),
            dma((9,)),
            dma((6,)),
            dma((6,)),
            dma((2, 2, n - 1)),
            dma((2, 2)),
            dma((2, 2, n - 1)),
            dma((2, 2)),
            dma((2, 2)),
            dma((2, 2)),
        ],
        compiler_params=pltpu.CompilerParams(
            collective_id=0, has_side_effects=True, vmem_limit_bytes=63 * 1024 * 1024
        ),
    )(
        tgt_basis,
        proj_basis,
        quad_weight.reshape(1, points),
        tgt_energy.reshape(1, rows),
        proj_energy,
        pair_flags.T,
        tile_counts.T,
        tgt_amp,
        proj_amp,
    )


def power_of_two(value):
    return value & (value - 1) == 0


def solution(mesh):
    in_specs = (
        P(None, "tgt", "rep"),
        P(None, None, "prj", "rep"),
        P(("bpar", "rep")),
        P(("tgt", "prj", "rep")),
        P(("tgt", "rep"), "prj"),
        P("bpar", None),
        P("bpar", None),
        P(("bpar", "tgt", "prj", "rep"), None),
        P(("bpar", "tgt", "rep"), "prj", None),
    )
    out_specs = (P(("bpar", "tgt", "prj", "rep"), None), P(("bpar", "tgt", "rep"), "prj", None))
    n_tgt, n_prj = mesh.shape["tgt"], mesh.shape["prj"]
    if power_of_two(n_tgt) and power_of_two(n_prj) and n_tgt * n_prj <= 8:
        body = functools.partial(kernel_shards, n_tgt, n_prj)
    else:
        body = shards
    return jax.shard_map(body, mesh=mesh, in_specs=in_specs, out_specs=out_specs, check_vma=False)
```
